32 devices in a mesh: shard: 2 (over core), tensor: 4 (over y, x), section: 4 (over z).
Axes of the slice: x: 2, y: 2, z: 4, core: 2. Of those that a mesh axis runs over, the one named last changes fastest.
Arguments:
- gradient: bfloat16 [6, 2048, 8192], P(None, ('tensor', 'section'), 'shard'), may hold values from -6 to 6
- basis: bfloat16 [6, 2048, 256], P(None, ('tensor', 'section')), may hold values from -6 to 6
- moment_m: float32 [6, 8192, 256], P(None, ('shard', 'tensor', 'section')), may hold values from -4 to 4
- moment_v: float32 [6, 8192, 256], P(None, ('shard', 'tensor', 'section')), may hold values from 0.002 to 0.02
Outputs:
- delta: bfloat16 [6, 2048, 8192], P(None, ('tensor', 'section'), 'shard')
- basis_new: bfloat16 [6, 2048, 256], P(None, ('tensor', 'section'))
- moment_m_new: float32 [6, 8192, 256], P(None, ('shard', 'tensor', 'section'))
- moment_v_new: float32 [6, 8192, 256], P(None, ('shard', 'tensor', 'section'))
The draws below stay inside these ranges and needn't reach their ends.
All inputs are finite; a program needn't handle non-finite values. Where the reference program divides by a largest or mean magnitude, that divisor is 1e-20 or more.
Results may differ from the reference program's by a relative error of at most 0.0049.
Values may be sent and summed in bfloat16 or wider, within the bound.
No kernel may reach another device: no remote copies, remote signals or barrier semaphores. Data moves between devices by JAX's collectives and lax.ppermute only.
A program may use at most 128 MiB of HBM per device.

```python
import math
import jax
import jax.numpy as jnp
from jax import lax

D = 2048
FF = 8192
RANK = 256
NS_ITERS = 4
NMAT = 6


def raised(result, rng, source, target, parts, factor):
    owner, partner = [(jnp.arange(result.shape[dim]) // (result.shape[dim] // parts)).reshape([-1 if axis == dim else 1 for axis in range(result.ndim)]) for dim in (source, target)]
    chosen = jax.random.permutation(rng, parts)[partner]
    strong = (owner == chosen) | (owner == (partner + parts // 2) % parts)
    return jnp.where(strong, factor * result, result)


def levels(key, shape, shards, least, high):
    def one(axis_at, blocks):
        steps = jax.random.uniform(jax.random.fold_in(jax.random.fold_in(key, 6), axis_at), (blocks,), jnp.float32, least / len(shards), high / len(shards))
        return jnp.repeat(jnp.exp(steps), shape[axis_at] // blocks).reshape((-1,) + (1,) * (len(shape) - axis_at - 1))

    level = one(*shards[0])
    for cut in shards[1:]:
        level = level * one(*cut)
    return level


def bell_draw(rng, dims, deviation, reach, split=(), kind=jnp.bfloat16):
    values = deviation * jax.random.normal(rng, dims, jnp.float32)
    if split:
        values = values * levels(rng, dims, split, -0.22, 0.18)
    return jnp.clip(values, -reach, reach).astype(kind)


def noise_with(rng, dims, spread, bound, pieces, heavy, kind=jnp.bfloat16):
    drawn = spread * jax.random.normal(rng, dims, jnp.float32)
    if pieces:
        drawn = drawn * levels(rng, dims, pieces, -0.22, 0.18)
    return jnp.clip(raised(drawn, jax.random.fold_in(rng, 3), *heavy), -bound, bound).astype(kind)


def setup_inputs(seed: int = 0) -> dict:
    arg_keys = jax.random.split(jax.random.key(seed), 5)
    gradient = noise_with(arg_keys[0], (NMAT, D, FF), 1.0, 6.0, ((1, 16), (2, 2)), (1, 2, 16, 2.0))
    basis = bell_draw(arg_keys[1], (NMAT, D, RANK), 1.0, 6.0, ((1, 16),))
    moment_m = bell_draw(arg_keys[2], (NMAT, FF, RANK), 0.5, 4.0, ((1, 32),), jnp.float32)
    moment_v = jnp.clip(jnp.exp(math.log(0.02) - 2.30258502 * jax.random.uniform(arg_keys[3], (NMAT, FF, RANK), jnp.float32) ** levels(arg_keys[3], (NMAT, FF, RANK), ((1, 32),), -0.2, 0.2)), 0.002, 0.02)
    return dict(gradient=gradient, basis=basis, moment_m=moment_m, moment_v=moment_v)


beta_one = 0.9
beta_two = 0.999
bias_one = 1.0 - 0.9 ** 10
bias_two = 1.0 - 0.999 ** 10
eps_adam = 1e-08
galore_gain = 4.0

def reference(gradient, basis, moment_m, moment_v):
    width_root = math.sqrt(D)
    grad_float = gradient.astype(jnp.float32)
    basis_float = basis.astype(jnp.float32)
    low_rank = jnp.einsum('kmn,kmr->knr', grad_float, basis_float) / width_root
    moment_m_new = beta_one * moment_m + (1.0 - beta_one) * low_rank
    moment_v_new = beta_two * moment_v + (1.0 - beta_two) * low_rank * low_rank
    step_low = (moment_m_new / bias_one / (jnp.sqrt(moment_v_new / bias_two) + eps_adam)).astype(jnp.bfloat16)
    delta = (-galore_gain / width_root * jnp.einsum('kmr,knr->kmn', basis_float, step_low.astype(jnp.float32))).astype(jnp.bfloat16)
    rough_low = low_rank.astype(jnp.bfloat16)
    subspace = jnp.einsum('kmn,knr->kmr', grad_float, rough_low.astype(jnp.float32))
    gram_mat = jnp.einsum('kmr,kms->krs', subspace, subspace, precision=lax.Precision.HIGHEST)
    row_bound = lax.optimization_barrier(jnp.max(lax.optimization_barrier(jnp.sum(jnp.abs(gram_mat), axis=2)), axis=1))[:, None, None] + 1e-06
    iterate = subspace / jnp.sqrt(row_bound)
    gram_mat = gram_mat / row_bound
    identity = jnp.eye(RANK, dtype=jnp.float32)
    for turn_index in range(NS_ITERS):
        factor = 1.5 * identity - 0.5 * gram_mat
        iterate = jnp.einsum('kmr,krs->kms', iterate, factor, precision=lax.Precision.HIGHEST)
        gram_mat = jnp.einsum('kmr,kms->krs', iterate, iterate, precision=lax.Precision.HIGHEST)
    basis_new = (width_root * iterate).astype(jnp.bfloat16)
    return (delta, basis_new, moment_m_new, moment_v_new)
```

```python
import functools
import math

import jax
import jax.numpy as jnp
from jax import lax
from jax.experimental import pallas as pl
from jax.experimental.pallas import tpu as pltpu
from jax.sharding import PartitionSpec as P

D = 2048
NS_ITERS = 4
CHUNKS = (2, 2, 2)
VMEM_LIMIT = 40 * 1024 * 1024

beta_one = 0.9
beta_two = 0.999
bias_one = 1.0 - 0.9**10
bias_two = 1.0 - 0.999**10
eps_adam = 1e-08
galore_gain = 4.0
width_root = math.sqrt(D)

F32 = jnp.float32
BF16 = jnp.bfloat16


def dot_tn(a, b):
    return lax.dot_general(a, b, (((0,), (0,)), ((), ())), preferred_element_type=F32)


def dot_nn(a, b):
    return lax.dot_general(a, b, (((1,), (0,)), ((), ())), preferred_element_type=F32)


def dot_nt(a, b):
    return lax.dot_general(a, b, (((1,), (1,)), ((), ())), preferred_element_type=F32)


def split(a):
    high = a.astype(BF16)
    return high, (a - high.astype(F32)).astype(BF16)


def fine(dot, a, b):
    (ah, al), (bh, bl) = a, b
    return dot(ah, bh) + (dot(ah, bl) + dot(al, bh))


def call(body, grid, prefetch, ins, outs, scratch, flops, aliases=None):
    moved = sum(math.prod(s) * jnp.dtype(d).itemsize for s, d, _, _ in outs)
    moved += sum(a.size * a.dtype.itemsize for a, b, _ in ins if b is not None)
    return pl.pallas_call(
        body,
        grid_spec=pltpu.PrefetchScalarGridSpec(
            num_scalar_prefetch=1,
            grid=grid,
            in_specs=[
                pl.BlockSpec(memory_space=pl.ANY) if b is None else pl.BlockSpec(b, m)
                for _, b, m in ins
            ],
            out_specs=[pl.BlockSpec(b, m) for _, _, b, m in outs],
            scratch_shapes=scratch,
        ),
        out_shape=[jax.ShapeDtypeStruct(s, d) for s, d, _, _ in outs],
        input_output_aliases=aliases or {},
        compiler_params=pltpu.CompilerParams(vmem_limit_bytes=VMEM_LIMIT),
        cost_estimate=pl.CostEstimate(flops=flops, bytes_accessed=moved, transcendentals=0),
    )(prefetch, *[a for a, _, _ in ins])


def low_partial(place, grads, bases, k0, kc, sections):
    rows, width = grads[0].shape[1:]
    rank = bases[0].shape[2]
    part = width // sections
    n = len(grads)

    def body(place_ref, *refs):
        g, b, out, total = refs[:n], refs[n : 2 * n], refs[2 * n : -1], refs[-1]
        acc = dot_tn(g[0][0], b[0][0])
        for m in range(1, n):
            acc += dot_tn(g[m][0], b[m][0])
        total[...] = acc
        for j in range(sections):
            at = pl.multiple_of(jnp.bitwise_xor(place_ref[1], j) * part, part)
            out[j][0] = total[pl.ds(at, part), :].astype(BF16)

    return call(
        body,
        (kc,),
        place,
        [(g, (1, rows, width), lambda i, p: (i, 0, 0)) for g in grads]
        + [(b, (1, rows, rank), lambda i, p: (k0 + i, 0, 0)) for b in bases],
        [((kc, part, rank), BF16, (1, part, rank), lambda i, p: (i, 0, 0))] * sections,
        [pltpu.VMEM((width, rank), F32)],
        2 * kc * n * rows * width * rank,
    )


def subspace_partial(place, grads, roughs, split_cores):
    kc, rows, width = grads[0].shape
    part, rank = roughs[0].shape[1:]
    n, s = len(grads), len(roughs)
    half = kc // 2

    def pick(i, p):
        if not split_cores:
            return (i, 0, 0)
        core = p[2]
        return (jnp.where(i < half, 2 * i + core, 2 * (i - half) + 1 - core), 0, 0)

    def body(place_ref, *refs):
        g, r, out, whole = refs[:n], refs[n : n + s], refs[n + s], refs[-1]
        for j in range(s):
            at = pl.multiple_of(jnp.bitwise_xor(place_ref[1], j) * part, part)
            whole[pl.ds(at, part), :] = r[j][0]
        for m in range(n):
            out[0, m] = dot_nn(g[m][0], whole[...])

    return call(
        body,
        (kc,),
        place,
        [(g, (1, rows, width), pick) for g in grads]
        + [(r, (1, part, rank), pick) for r in roughs],
        [((kc, n, rows, rank), F32, (1, n, rows, rank), lambda i, p: (i, 0, 0, 0))],
        [pltpu.VMEM((width, rank), BF16)],
        2 * kc * n * rows * width * rank,
    )[0]


def delta_parts(place, bases, steps, k0):
    kc, part, rank = steps[0].shape
    rows = bases[0].shape[1]
    n, s = len(bases), len(steps)
    width = part * s

    def body(place_ref, *refs):
        b, r, out, whole = refs[:n], refs[n : n + s], refs[n + s : -1], refs[-1]
        for j in range(s):
            at = pl.multiple_of(jnp.bitwise_xor(place_ref[1], j) * part, part)
            whole[pl.ds(at, part), :] = r[j][0]
        for m in range(n):
            out[m][0] = (-galore_gain / width_root * dot_nt(b[m][0], whole[...])).astype(BF16)

    return call(
        body,
        (kc,),
        place,
        [(b, (1, rows, rank), lambda i, p: (k0 + i, 0, 0)) for b in bases]
        + [(r, (1, part, rank), lambda i, p: (i, 0, 0)) for r in steps],
        [((kc, rows, width), BF16, (1, rows, width), lambda i, p: (i, 0, 0))] * n,
        [pltpu.VMEM((width, rank), BF16)],
        2 * kc * n * rows * width * rank,
    )


def place_delta(place, parts, before, k0, matrices):
    kc, rows, width = parts[0].shape
    n = len(parts)

    def body(place_ref, *refs):
        out = refs[-1]
        for m in range(n):
            at = pl.multiple_of(jnp.bitwise_xor(place_ref[0], m) * width, width)
            out[0, :, pl.ds(at, width)] = refs[m][0]

    ins = [(p, (1, rows, width), lambda i, p: (i, 0, 0)) for p in parts]
    aliases = {}
    if before is not None:
        ins.append((before, None, None))
        aliases = {n + 1: 0}
    return call(
        body,
        (kc,),
        place,
        ins,
        [
            (
                (matrices, rows, n * width),
                BF16,
                (1, rows, n * width),
                lambda i, p: (k0 + i, 0, 0),
            )
        ],
        [],
        0,
        aliases,
    )[0]


def gram_parts(place, groups):
    n = len(groups[0])
    rows, rank = groups[0][0].shape[1:]
    counts = [g[0].shape[0] for g in groups]
    total = sum(counts)
    part = rank // n
    flat = [p for g in groups for p in g]

    def body(place_ref, *refs):
        pieces, sub, out, whole = refs[: len(flat)], refs[len(flat)], refs[len(flat) + 1 : -1], refs[-1]
        at = 0
        for j, count in enumerate(counts):
            for i in range(count):
                acc = pieces[j * n][i]
                for m in range(1, n):
                    acc += pieces[j * n + m][i]
                sub[at] = acc
                high = split(acc)
                whole[at] = fine(dot_tn, high, high)
                at += 1
        for m in range(n):
            start = pl.multiple_of(jnp.bitwise_xor(place_ref[0], m) * part, part)
            for i in range(total):
                out[m][i] = whole[i, pl.ds(start, part), :]

    zero3 = lambda i, p: (0, 0, 0)
    res = call(
        body,
        (1,),
        place,
        [(p, p.shape, zero3) for p in flat],
        [((total, rows, rank), F32, (total, rows, rank), zero3)]
        + [((total, part, rank), F32, (total, part, rank), zero3)] * n,
        [pltpu.VMEM((total, rank, rank), F32)],
        6 * total * rows * rank * rank,
    )
    return res[0], res[1:]


def newton_schulz(place, pieces, sub):
    n = len(pieces)
    total, rows, rank = sub.shape
    part = rank // n

    def body(place_ref, *refs):
        p, s, out, whole = refs[:n], refs[n], refs[n + 1], refs[-1]
        for m in range(n):
            start = pl.multiple_of(jnp.bitwise_xor(place_ref[0], m) * part, part)
            for i in range(total):
                whole[i, pl.ds(start, part), :] = p[m][i]
        row = lax.broadcasted_iota(jnp.int32, (rank, rank), 0)
        col = lax.broadcasted_iota(jnp.int32, (rank, rank), 1)
        eye = jnp.where(row == col, 1.0, 0.0).astype(F32)
        iters, grams, prods = [], [], []
        for i in range(total):
            gram = whole[i]
            bound = jnp.max(jnp.sum(jnp.abs(gram), axis=1, keepdims=True), axis=0, keepdims=True) + 1e-06
            iters.append(s[i] / jnp.sqrt(bound))
            grams.append(gram / bound)
            prods.append(None)
        for turn in range(NS_ITERS):
            for i in range(total):
                factor = 1.5 * eye - 0.5 * grams[i]
                f = split(factor)
                prods[i] = factor if turn == 0 else fine(dot_nn, split(prods[i]), f)
                if turn + 1 < NS_ITERS:
                    half = fine(dot_nn, split(grams[i]), f)
                    grams[i] = fine(dot_nn, split(half), f)
        for i in range(total):
            res = fine(dot_nn, split(iters[i]), split(prods[i]))
            out[i] = (width_root * res).astype(BF16)

    zero3 = lambda i, p: (0, 0, 0)
    return call(
        body,
        (1,),
        place,
        [(p, p.shape, zero3) for p in pieces] + [(sub, sub.shape, zero3)],
        [((total, rows, rank), BF16, (total, rows, rank), zero3)],
        [pltpu.VMEM((total, rank, rank), F32)],
        60 * total * rank * rank * rank,
    )[0]


def per_device(shape, gradient, basis, moment_m, moment_v):
    tensors, sections, cores = shape["tensor"], shape["section"], shape["shard"]
    t, z, c = (lax.axis_index(a) for a in ("tensor", "section", "shard"))
    place = jnp.stack([t, z, c]).astype(jnp.int32)
    matrices, rows, columns = gradient.shape
    width = columns // tensors
    split_cores = cores == 2

    def swap(x, axis, m):
        return lax.ppermute(x, axis, [(i, i ^ m) for i in range(shape[axis])])

    def other_core(x):
        return lax.ppermute(x, "shard", [(0, 1), (1, 0)])

    if split_cores:
        mine = lax.dynamic_slice_in_dim(basis, c * (matrices // 2), matrices // 2, 0)
        got = jnp.stack([swap(mine, "tensor", m) for m in range(1, tensors)])
        theirs = other_core(got)
        first = jnp.where(c == 0, got, theirs)
        second = jnp.where(c == 0, theirs, got)
        bases = [basis] + [
            jnp.concatenate([first[m], second[m]], 0) for m in range(tensors - 1)
        ]
    else:
        bases = [basis] + [swap(basis, "tensor", m) for m in range(1, tensors)]

    starts = [sum(CHUNKS[:j]) for j in range(len(CHUNKS))]
    grads, lows = [], []
    for k0, kc in zip(starts, CHUNKS):
        cut = [
            lax.dynamic_slice(gradient, (k0, 0, (t ^ m) * width), (kc, rows, width))
            for m in range(tensors)
        ]
        grads.append([cut[0]] + [swap(cut[m], "tensor", m) for m in range(1, tensors)])

    m_news, v_news, steps, groups = [], [], [], []
    for j, (k0, kc) in enumerate(zip(starts, CHUNKS)):
        parts = low_partial(place, grads[j], bases, k0, kc, sections)
        total = parts[0].astype(F32)
        for m in range(1, sections):
            total += swap(parts[m], "section", m).astype(F32)
        low_rank = total / width_root
        m_new = beta_one * moment_m[k0 : k0 + kc] + (1.0 - beta_one) * low_rank
        v_new = beta_two * moment_v[k0 : k0 + kc] + (1.0 - beta_two) * low_rank * low_rank
        step_low = (m_new / bias_one / (jnp.sqrt(v_new / bias_two) + eps_adam)).astype(BF16)
        rough_low = low_rank.astype(BF16)
        m_news.append(m_new)
        v_news.append(v_new)
        roughs = [rough_low] + [swap(rough_low, "section", m) for m in range(1, sections)]
        steps.append([step_low] + [swap(step_low, "section", m) for m in range(1, sections)])
        sub = subspace_partial(place, grads[j], roughs, split_cores)
        if split_cores:
            half = kc // 2
            sub = sub[:half] + other_core(sub[half:])
        else:
            sub = lax.psum(sub, "shard")
        groups.append([sub[:, 0]] + [swap(sub[:, m], "tensor", m) for m in range(1, tensors)])

    sub, cut = gram_parts(place, groups)
    gram = cut[0]
    for m in range(1, tensors):
        gram = gram + swap(cut[m], "tensor", m)
    pieces = [gram] + [swap(gram, "section", m) for m in range(1, sections)]
    gram = functools.reduce(jnp.add, pieces)
    pieces = [gram] + [swap(gram, "tensor", m) for m in range(1, tensors)]
    done = newton_schulz(place, pieces, sub)
    if split_cores:
        theirs = other_core(done)
        even = jnp.where(c == 0, done, theirs)
        odd = jnp.where(c == 0, theirs, done)
        basis_new = jnp.stack([even, odd], 1).reshape(basis.shape)
    else:
        basis_new = done

    delta = None
    for j, k0 in enumerate(starts):
        cut = delta_parts(place, bases, steps[j], k0)
        parts = [cut[0]] + [swap(cut[m], "tensor", m) for m in range(1, tensors)]
        delta = place_delta(place, parts, delta, k0, matrices)

    return (delta, basis_new, jnp.concatenate(m_news, 0), jnp.concatenate(v_news, 0))


def solution(mesh):
    placed = (
        P(None, ("tensor", "section"), "shard"),
        P(None, ("tensor", "section"), None),
        P(None, ("shard", "tensor", "section"), None),
        P(None, ("shard", "tensor", "section"), None),
    )
    return jax.shard_map(
        functools.partial(per_device, dict(mesh.shape)),
        mesh=mesh,
        in_specs=placed,
        out_specs=placed,
        check_vma=False,
    )
```

```python
import functools
import math

import jax
import jax.numpy as jnp
from jax import lax
from jax.experimental import pallas as pl
from jax.experimental.pallas import tpu as pltpu
from jax.sharding import PartitionSpec as P

D = 2048
NS_ITERS = 4
CHUNKS = (2, 2, 2)
VMEM_LIMIT = 40 * 1024 * 1024

beta_one = 0.9
beta_two = 0.999
bias_one = 1.0 - 0.9**10
bias_two = 1.0 - 0.999**10
eps_adam = 1e-08
galore_gain = 4.0
width_root = math.sqrt(D)

F32 = jnp.float32
BF16 = jnp.bfloat16


def dot_tn(a, b):
    return lax.dot_general(a, b, (((0,), (0,)), ((), ())), preferred_element_type=F32)


def dot_nn(a, b):
    return lax.dot_general(a, b, (((1,), (0,)), ((), ())), preferred_element_type=F32)


def dot_nt(a, b):
    return lax.dot_general(a, b, (((1,), (1,)), ((), ())), preferred_element_type=F32)


def split(a):
    high = a.astype(BF16)
    return high, (a - high.astype(F32)).astype(BF16)


def fine(dot, a, b):
    (ah, al), (bh, bl) = a, b
    return dot(ah, bh) + (dot(ah, bl) + dot(al, bh))


def call(body, grid, prefetch, ins, outs, scratch, flops, aliases=None):
    moved = sum(math.prod(s) * jnp.dtype(d).itemsize for s, d, _, _ in outs)
    moved += sum(a.size * a.dtype.itemsize for a, b, _ in ins if b is not None)
    return pl.pallas_call(
        body,
        grid_spec=pltpu.PrefetchScalarGridSpec(
            num_scalar_prefetch=1,
            grid=grid,
            in_specs=[
                pl.BlockSpec(memory_space=pl.ANY) if b is None else pl.BlockSpec(b, m)
                for _, b, m in ins
            ],
            out_specs=[pl.BlockSpec(b, m) for _, _, b, m in outs],
            scratch_shapes=scratch,
        ),
        out_shape=[jax.ShapeDtypeStruct(s, d) for s, d, _, _ in outs],
        input_output_aliases=aliases or {},
        compiler_params=pltpu.CompilerParams(vmem_limit_bytes=VMEM_LIMIT),
        cost_estimate=pl.CostEstimate(flops=1, bytes_accessed=1, transcendentals=0),
    )(prefetch, *[a for a, _, _ in ins])


def outgoing(place, gradient, basis, k0, kc, tensors, after):
    rows, columns = gradient.shape[1:]
    rank = basis.shape[2]
    width = columns // tensors
    n = tensors - 1

    def body(place_ref, *refs):
        g, b, out = refs[:n], refs[n], refs[-n:]
        for m in range(n):
            out[m][0, :, :width] = g[m][0]
            out[m][0, :, width:] = b[0]

    return call(
        body,
        (kc,),
        place,
        [
            (gradient, (1, rows, width), lambda i, p, m=m: (k0 + i, 0, jnp.bitwise_xor(p[0], m)))
            for m in range(1, tensors)
        ]
        + [(basis, (1, rows, rank), lambda i, p: (k0 + i, 0, 0))]
        + [(a, None, None) for a in after],
        [((kc, rows, width + rank), BF16, (1, rows, width + rank), lambda i, p: (i, 0, 0))] * n,
        [],
        0,
    )


def sources(gradient, basis, got, k0, pick=lambda i, p: i):
    rows, rank = basis.shape[1:]
    kc, _, wide = got[0].shape
    return [
        (gradient, (1, rows, wide - rank), lambda i, p: (k0 + pick(i, p), 0, p[0])),
        (basis, (1, rows, rank), lambda i, p: (k0 + pick(i, p), 0, 0)),
    ] + [(g, (1, rows, wide), lambda i, p: (pick(i, p), 0, 0)) for g in got]


def low_partial(place, gradient, basis, got, k0, sections):
    rows, rank = basis.shape[1:]
    kc, _, wide = got[0].shape
    width = wide - rank
    part = width // sections
    n = len(got)
    chosen = blocks_sent(sections)

    def body(place_ref, *refs):
        out, total = refs[2 + n : -1], refs[-1]
        acc = dot_tn(refs[0][0], refs[1][0])
        for m in range(n):
            acc += dot_tn(refs[2 + m][0, :, :width], refs[2 + m][0, :, width:])
        total[...] = acc
        z = place_ref[1]
        for j, block in enumerate(chosen):
            at = pl.multiple_of(block(z) * part, part)
            out[j][0] = total[pl.ds(at, part), :].astype(out[j].dtype)

    return call(
        body,
        (kc,),
        place,
        sources(gradient, basis, got, k0),
        [
            ((kc, part, rank), BF16 if j else F32, (1, part, rank), lambda i, p: (i, 0, 0))
            for j in range(len(chosen))
        ],
        [pltpu.VMEM((width, rank), F32)],
        2 * kc * (n + 1) * rows * width * rank,
    )


def blocks_sent(sections):
    return [lambda z, m=m: jnp.bitwise_xor(z, m) for m in range(sections)]


def section_sum(parts, swap):
    if len(parts) != 4:
        return [parts[0]] + [swap(parts[m], "section", m) for m in range(1, len(parts))]
    own, near, two, far = parts
    far = swap(far, "section", 1)
    near = swap(near, "section", 1)
    two = (two.astype(F32) + far.astype(F32)).astype(BF16)
    return [own, near, swap(two, "section", 2)]


def section_gather(x, sections, swap):
    if sections != 4:
        return [x] + [swap(x, "section", m) for m in range(1, sections)]
    two = swap(x, "section", 2)
    near = swap(x, "section", 1)
    return [x, near, two, swap(two, "section", 1)]


def gather_into(whole, refs, z):
    part = refs[0].shape[-2]
    for j, ref in enumerate(refs):
        at = pl.multiple_of(jnp.bitwise_xor(z, j) * part, part)
        whole[pl.ds(at, part), :] = ref[0]


def update(place, terms, moment_m, moment_v, before, k0):
    kc, part, rank = terms[0].shape
    n = len(terms)

    def body(place_ref, *refs):
        m_ref, v_ref = refs[n], refs[n + 1]
        rough, step_out, m_out, v_out = refs[-4:]
        total = refs[0][0]
        for j in range(1, n):
            total += refs[j][0].astype(F32)
        low_rank = total / width_root
        m_new = beta_one * m_ref[0] + (1.0 - beta_one) * low_rank
        v_new = beta_two * v_ref[0] + (1.0 - beta_two) * low_rank * low_rank
        step = m_new / bias_one / (jnp.sqrt(v_new / bias_two) + eps_adam)
        rough[0] = low_rank.astype(BF16)
        step_out[0] = step.astype(BF16)
        m_out[0] = m_new
        v_out[0] = v_new

    here = lambda i, p: (k0 + i, 0, 0)
    block = (1, part, rank)
    ins = [(a, block, lambda i, p: (i, 0, 0)) for a in terms]
    ins += [(moment_m, block, here), (moment_v, block, here)]
    aliases = {}
    if before is not None:
        ins += [(b, None, None) for b in before]
        aliases = {n + 3: 2, n + 4: 3}
    return call(
        body,
        (kc,),
        place,
        ins,
        [
            ((kc, part, rank), BF16, block, lambda i, p: (i, 0, 0)),
            ((kc, part, rank), BF16, block, lambda i, p: (i, 0, 0)),
            (moment_m.shape, F32, block, here),
            (moment_v.shape, F32, block, here),
        ],
        [],
        0,
        aliases,
    )


def subspace_partial(place, gradient, basis, got, gathered, k0, split_cores):
    rows, rank = basis.shape[1:]
    kc, _, wide = got[0].shape
    width = wide - rank
    part = gathered[0].shape[1]
    n, s = len(got), len(gathered)
    half = kc // 2

    def pick(i, p):
        if not split_cores:
            return i
        return jnp.where(i < half, 2 * i + p[2], 2 * (i - half) + 1 - p[2])

    def body(place_ref, *refs):
        out, whole = refs[-2:]
        gather_into(whole, refs[2 + n : 2 + n + s], place_ref[1])
        out[0, 0] = dot_nn(refs[0][0], whole[...])
        for m in range(n):
            out[0, m + 1] = dot_nn(refs[2 + m][0, :, :width], whole[...])

    return call(
        body,
        (kc,),
        place,
        sources(gradient, basis, got, k0, pick)
        + [(r, (1, part, rank), lambda i, p: (pick(i, p), 0, 0)) for r in gathered],
        [((kc, n + 1, rows, rank), F32, (1, n + 1, rows, rank), lambda i, p: (i, 0, 0, 0))],
        [pltpu.VMEM((width, rank), BF16)],
        2 * kc * (n + 1) * rows * width * rank,
    )[0]


def delta_parts(place, basis, got, gathered, k0):
    rows, rank = basis.shape[1:]
    kc, _, wide = got[0].shape
    width = wide - rank
    part = gathered[0].shape[1]
    n, s = len(got), len(gathered)

    def body(place_ref, *refs):
        out, whole = refs[1 + n + s : -1], refs[-1]
        gather_into(whole, refs[1 + n : 1 + n + s], place_ref[1])
        for m in range(n + 1):
            b = refs[m][0, :, width:] if m else refs[0][0]
            out[m][0] = (-galore_gain / width_root * dot_nt(b, whole[...])).astype(BF16)

    return call(
        body,
        (kc,),
        place,
        [(basis, (1, rows, rank), lambda i, p: (k0 + i, 0, 0))]
        + [(g, (1, rows, wide), lambda i, p: (i, 0, 0)) for g in got]
        + [(r, (1, part, rank), lambda i, p: (i, 0, 0)) for r in gathered],
        [((kc, rows, width), BF16, (1, rows, width), lambda i, p: (i, 0, 0))] * (n + 1),
        [pltpu.VMEM((width, rank), BF16)],
        2 * kc * (n + 1) * rows * width * rank,
    )


def place_delta(place, parts, before, k0, matrices):
    kc, rows, width = parts[0].shape
    n = len(parts)

    def body(place_ref, *refs):
        out = refs[-1]
        for m in range(n):
            at = pl.multiple_of(jnp.bitwise_xor(place_ref[0], m) * width, width)
            out[0, :, pl.ds(at, width)] = refs[m][0]

    ins = [(p, (1, rows, width), lambda i, p: (i, 0, 0)) for p in parts]
    aliases = {}
    if before is not None:
        ins.append((before, None, None))
        aliases = {n + 1: 0}
    shape = (matrices, rows, n * width)
    return call(
        body,
        (kc,),
        place,
        ins,
        [(shape, BF16, (1, rows, n * width), lambda i, p: (k0 + i, 0, 0))],
        [],
        0,
        aliases,
    )[0]


def gram_parts(place, groups):
    n = len(groups[0])
    rows, rank = groups[0][0].shape[1:]
    counts = [g[0].shape[0] for g in groups]
    total = sum(counts)
    part = rank // n
    flat = [p for g in groups for p in g]

    def body(place_ref, *refs):
        pieces, sub, out, whole = refs[: len(flat)], refs[len(flat)], refs[len(flat) + 1 : -1], refs[-1]
        at = 0
        for j, count in enumerate(counts):
            for i in range(count):
                acc = pieces[j * n][i]
                for m in range(1, n):
                    acc += pieces[j * n + m][i]
                sub[at] = acc
                high = split(acc)
                whole[at] = fine(dot_tn, high, high)
                at += 1
        for m in range(n):
            start = pl.multiple_of(jnp.bitwise_xor(place_ref[0], m) * part, part)
            for i in range(total):
                out[m][i] = whole[i, pl.ds(start, part), :]

    zero3 = lambda i, p: (0, 0, 0)
    res = call(
        body,
        (1,),
        place,
        [(p, p.shape, zero3) for p in flat],
        [((total, rows, rank), F32, (total, rows, rank), zero3)]
        + [((total, part, rank), F32, (total, part, rank), zero3)] * n,
        [pltpu.VMEM((total, rank, rank), F32)],
        6 * total * rows * rank * rank,
    )
    return res[0], res[1:]


def newton_schulz(place, pieces, sub):
    n = len(pieces)
    total, rows, rank = sub.shape
    part = rank // n

    def body(place_ref, *refs):
        p, s, out, whole = refs[:n], refs[n], refs[n + 1], refs[-1]
        for m in range(n):
            start = pl.multiple_of(jnp.bitwise_xor(place_ref[0], m) * part, part)
            for i in range(total):
                whole[i, pl.ds(start, part), :] = p[m][i]
        row = lax.broadcasted_iota(jnp.int32, (rank, rank), 0)
        col = lax.broadcasted_iota(jnp.int32, (rank, rank), 1)
        eye = jnp.where(row == col, 1.0, 0.0).astype(F32)
        iters, grams, prods = [], [], []
        for i in range(total):
            gram = whole[i]
            bound = jnp.max(jnp.sum(jnp.abs(gram), axis=1, keepdims=True), axis=0, keepdims=True) + 1e-06
            iters.append(s[i] / jnp.sqrt(bound))
            grams.append(gram / bound)
            prods.append(None)
        for turn in range(NS_ITERS):
            for i in range(total):
                factor = 1.5 * eye - 0.5 * grams[i]
                f = split(factor)
                prods[i] = factor if turn == 0 else fine(dot_nn, split(prods[i]), f)
                if turn + 1 < NS_ITERS:
                    half = fine(dot_nn, split(grams[i]), f)
                    grams[i] = fine(dot_nn, split(half), f)
        for i in range(total):
            res = fine(dot_nn, split(iters[i]), split(prods[i]))
            out[i] = (width_root * res).astype(BF16)

    zero3 = lambda i, p: (0, 0, 0)
    return call(
        body,
        (1,),
        place,
        [(p, p.shape, zero3) for p in pieces] + [(sub, sub.shape, zero3)],
        [((total, rows, rank), BF16, (total, rows, rank), zero3)],
        [pltpu.VMEM((total, rank, rank), F32)],
        60 * total * rank * rank * rank,
    )[0]


def after(x, *others):
    return lax.optimization_barrier((x, others))[0]


def per_device(shape, gradient, basis, moment_m, moment_v):
    tensors, sections, cores = shape["tensor"], shape["section"], shape["shard"]
    t, z, c = (lax.axis_index(a) for a in ("tensor", "section", "shard"))
    place = jnp.stack([t, z, c]).astype(jnp.int32)
    matrices = gradient.shape[0]
    split_cores = cores == 2
    n = len(CHUNKS)
    starts = [sum(CHUNKS[:j]) for j in range(n)]

    def swap(x, axis, m):
        return lax.ppermute(x, axis, [(i, i ^ m) for i in range(shape[axis])])

    def other_core(x):
        return lax.ppermute(x, "shard", [(0, 1), (1, 0)])

    def swap_all(cut):
        return [swap(cut[m - 1], "tensor", m) for m in range(1, tensors)]

    def then(*values):
        nonlocal place
        place = after(place, *values)

    grads, roughs, steps, cuts, groups = {}, {}, {}, {}, {}
    rough_own, step_own, state = {}, {}, {"news": None, "delta": None}

    def send(j, *waits):
        cut = outgoing(place, gradient, basis, starts[j], CHUNKS[j], tensors, waits)
        grads[j] = swap_all(cut)
        then(cut)

    def low(j):
        parts = low_partial(place, gradient, basis, grads[j], starts[j], sections)
        then(parts)
        return section_sum(parts, swap)

    def step(j, terms):
        rough, new, *state["news"] = update(place, terms, moment_m, moment_v, state["news"], starts[j])
        rough_own[j], step_own[j] = rough, new
        then(rough)

    def subspace(j):
        sub = subspace_partial(place, gradient, basis, grads[j], roughs[j], starts[j], split_cores)
        then(sub)
        if split_cores:
            half = CHUNKS[j] // 2
            sub = sub[:half] + other_core(sub[half:])
        else:
            sub = lax.psum(sub, "shard")
        groups[j] = [sub[:, 0]] + [swap(sub[:, m], "tensor", m) for m in range(1, tensors)]

    def delta(j):
        cut = delta_parts(place, basis, grads[j], steps[j], starts[j])
        then(cut)
        cuts[j] = [cut[0]] + swap_all(cut[1:])

    def put(j):
        state["delta"] = place_delta(place, cuts[j], state["delta"], starts[j], matrices)
        then(state["delta"])

    def gather(x):
        return section_gather(x, sections, swap)

    send(0)
    send(1, *grads[0])
    terms = low(0)
    step(0, terms)
    roughs[0] = gather(rough_own[0])
    steps[0] = gather(step_own[0])
    send(2, *grads[1])
    terms = low(1)
    step(1, terms)
    subspace(0)
    delta(0)
    roughs[1] = gather(rough_own[1])
    steps[1] = gather(step_own[1])
    terms = low(2)
    step(2, terms)
    subspace(1)
    delta(1)
    put(0)
    roughs[2] = gather(rough_own[2])
    steps[2] = gather(after(step_own[2], roughs[2][2]))
    subspace(2)
    put(1)
    delta(2)
    sub, cut = gram_parts(place, [groups[j] for j in range(n)])
    then(sub)
    gram = cut[0]
    for m in range(1, tensors):
        gram = gram + swap(cut[m], "tensor", m)
    reach = 1
    while reach < sections:
        gram = gram + swap(gram, "section", reach)
        reach *= 2
    pieces = [gram] + [swap(gram, "tensor", m) for m in range(1, tensors)]
    done = newton_schulz(place, pieces, sub)
    then(done)
    if split_cores:
        theirs = other_core(done)
        even = jnp.where(c == 0, done, theirs)
        odd = jnp.where(c == 0, theirs, done)
        basis_new = jnp.stack([even, odd], 1).reshape(basis.shape)
    else:
        basis_new = done
    put(2)
    return (state["delta"], basis_new, *state["news"])


def solution(mesh):
    placed = (
        P(None, ("tensor", "section"), "shard"),
        P(None, ("tensor", "section"), None),
        P(None, ("shard", "tensor", "section"), None),
        P(None, ("shard", "tensor", "section"), None),
    )
    return jax.shard_map(
        functools.partial(per_device, dict(mesh.shape)),
        mesh=mesh,
        in_specs=placed,
        out_specs=placed,
        check_vma=False,
    )
```

```python
import functools
import math

import jax
import jax.numpy as jnp
from jax import lax
from jax.experimental import pallas as pl
from jax.experimental.pallas import tpu as pltpu
from jax.sharding import PartitionSpec as P

D = 2048
NS_ITERS = 4
CHUNKS = (2, 2, 2)
VMEM_LIMIT = 24 * 1024 * 1024

beta_one = 0.9
beta_two = 0.999
bias_one = 1.0 - 0.9**10
bias_two = 1.0 - 0.999**10
eps_adam = 1e-08
galore_gain = 4.0
width_root = math.sqrt(D)

F32 = jnp.float32
BF16 = jnp.bfloat16


def dot_tn(a, b):
    return lax.dot_general(a, b, (((0,), (0,)), ((), ())), preferred_element_type=F32)


def dot_nn(a, b):
    return lax.dot_general(a, b, (((1,), (0,)), ((), ())), preferred_element_type=F32)


def dot_nt(a, b):
    return lax.dot_general(a, b, (((1,), (1,)), ((), ())), preferred_element_type=F32)


def split(a):
    high = a.astype(BF16)
    return high, (a - high.astype(F32)).astype(BF16)


def fine(dot, a, b):
    (ah, al), (bh, bl) = a, b
    return dot(ah, bh) + (dot(ah, bl) + dot(al, bh))


def call(body, grid, prefetch, ins, outs, scratch, aliases=None, vmem=VMEM_LIMIT):
    return pl.pallas_call(
        body,
        grid_spec=pltpu.PrefetchScalarGridSpec(
            num_scalar_prefetch=1,
            grid=grid,
            in_specs=[
                pl.BlockSpec(memory_space=pl.ANY) if b is None else pl.BlockSpec(b, m)
                for _, b, m in ins
            ],
            out_specs=[pl.BlockSpec(b, m) for _, _, b, m in outs],
            scratch_shapes=scratch,
        ),
        out_shape=[jax.ShapeDtypeStruct(s, d) for s, d, _, _ in outs],
        input_output_aliases=aliases or {},
        compiler_params=pltpu.CompilerParams(vmem_limit_bytes=vmem),
        cost_estimate=pl.CostEstimate(flops=1, bytes_accessed=1, transcendentals=0),
    )(prefetch, *[a for a, _, _ in ins])


def outgoing(place, gradient, k0, kc, tensors):
    rows, columns = gradient.shape[1:]
    width = columns // tensors
    n = tensors - 1

    def body(place_ref, *refs):
        for m in range(n):
            refs[n + m][...] = refs[m][...]

    return call(
        body,
        (kc,),
        place,
        [
            (gradient, (1, rows, width), lambda i, p, m=m: (k0 + i, 0, jnp.bitwise_xor(p[0], m)))
            for m in range(1, tensors)
        ],
        [((kc, rows, width), BF16, (1, rows, width), lambda i, p: (i, 0, 0))] * n,
        [],
        vmem=60 * 1024 * 1024 if k0 == 0 else VMEM_LIMIT,
    )


def gradient_ins(gradient, got, k0, pick=lambda i, p: i):
    kc, rows, width = got[0].shape
    return [(gradient, (1, rows, width), lambda i, p: (k0 + pick(i, p), 0, p[0]))] + [
        (g, (1, rows, width), lambda i, p: (pick(i, p), 0, 0)) for g in got
    ]


def basis_ins(bases, k0):
    return [
        (a, (1,) + a.shape[1:], lambda i, p, n=a.shape[0]: (lax.rem(k0 + i, n), 0, 0))
        for group in bases
        for a in group
    ]


def basis_blocks(refs, bases, k0, core):
    refs = list(refs)
    blocks = []
    for group in bases:
        mine = refs.pop(0)[0]
        if len(group) == 2:
            owner = (k0 + pl.program_id(0)) // group[0].shape[0]
            mine = jnp.where(owner == core, mine, refs.pop(0)[0])
        blocks.append(mine)
    return blocks


def low_partial(place, gradient, bases, got, k0, sections):
    kc, rows, width = got[0].shape
    rank = bases[0][0].shape[2]
    part = width // sections
    n = len(bases)
    chosen = blocks_sent(sections)

    def body(place_ref, *refs):
        out, total = refs[-1 - len(chosen) : -1], refs[-1]
        blocks = basis_blocks(refs[n:], bases, k0, place_ref[2])
        acc = dot_tn(refs[0][0], blocks[0])
        for m in range(1, n):
            acc += dot_tn(refs[m][0], blocks[m])
        total[...] = acc
        z = place_ref[1]
        for j, block in enumerate(chosen):
            at = pl.multiple_of(block(z) * part, part)
            out[j][0] = total[pl.ds(at, part), :].astype(out[j].dtype)

    return call(
        body,
        (kc,),
        place,
        gradient_ins(gradient, got, k0) + basis_ins(bases, k0),
        [
            ((kc, part, rank), BF16 if j else F32, (1, part, rank), lambda i, p: (i, 0, 0))
            for j in range(len(chosen))
        ],
        [pltpu.VMEM((width, rank), F32)],
    )


def blocks_sent(sections):
    return [lambda z, m=m: jnp.bitwise_xor(z, m) for m in range(sections)]


def gather_into(whole, refs, gathered, z):
    refs = list(refs)
    part = refs[0].shape[-2]
    for j, group in enumerate(gathered):
        block = refs.pop(0)[0, 0]
        for _ in group[1:]:
            block = block + refs.pop(0)[0, 0]
        at = pl.multiple_of(jnp.bitwise_xor(z, j) * part, part)
        whole[pl.ds(at, part), :] = block


def update(place, terms, moment_m, moment_v, before, k0, joined):
    kc, part, rank = terms[0].shape
    n = len(terms)

    def body(place_ref, *refs):
        m_ref, v_ref = refs[n], refs[n + 1]
        *low_out, m_out, v_out = refs[-4 + joined :]
        total = refs[0][0]
        for j in range(1, n):
            total += refs[j][0].astype(F32)
        low_rank = total / width_root
        m_new = beta_one * m_ref[0] + (1.0 - beta_one) * low_rank
        v_new = beta_two * v_ref[0] + (1.0 - beta_two) * low_rank * low_rank
        step = m_new / bias_one / (jnp.sqrt(v_new / bias_two) + eps_adam)
        low_out[0][0, 0] = low_rank.astype(BF16)
        low_out[-1][int(joined), 0] = step.astype(BF16)
        m_out[0] = m_new
        v_out[0] = v_new

    here = lambda i, p: (k0 + i, 0, 0)
    block = (1, part, rank)
    ins = [(a, block, lambda i, p: (i, 0, 0)) for a in terms]
    ins += [(moment_m, block, here), (moment_v, block, here)]
    aliases = {}
    if before is not None:
        ins += [(b, None, None) for b in before]
        aliases = {n + 3: 2 - joined, n + 4: 3 - joined}
    return call(
        body,
        (kc,),
        place,
        ins,
        [
            (
                (1 + joined, kc, part, rank),
                BF16,
                (1 + joined, 1, part, rank),
                lambda i, p: (0, i, 0, 0),
            )
        ]
        * (2 - joined)
        + [
            (moment_m.shape, F32, block, here),
            (moment_v.shape, F32, block, here),
        ],
        [],
        aliases,
    )


def subspace_partial(place, gradient, got, gathered, k0, split_cores):
    kc, rows, width = got[0].shape
    flat = [r for group in gathered for r in group]
    part, rank = flat[0].shape[2:]
    n, s = len(got) + 1, len(flat)
    half = kc // 2

    def pick(i, p):
        if not split_cores:
            return i
        return jnp.where(i < half, 2 * i + p[2], 2 * (i - half) + 1 - p[2])

    def body(place_ref, *refs):
        out, whole = refs[-2:]
        gather_into(whole, refs[n : n + s], gathered, place_ref[1])
        for m in range(n):
            out[0, m] = dot_nn(refs[m][0], whole[...])

    return call(
        body,
        (kc,),
        place,
        gradient_ins(gradient, got, k0, pick)
        + [(r, (1, 1, part, rank), lambda i, p: (0, pick(i, p), 0, 0)) for r in flat],
        [((kc, n, rows, rank), F32, (1, n, rows, rank), lambda i, p: (i, 0, 0, 0))],
        [pltpu.VMEM((width, rank), BF16)],
    )[0]


def delta_parts(place, bases, gathered, k0):
    flat = [r for group in gathered for r in group]
    kc, part, rank = flat[0].shape[1:]
    rows = bases[0][0].shape[1]
    n, s = len(bases), len(flat)
    width = part * len(gathered)

    def body(place_ref, *refs):
        out, whole = refs[-1 - n : -1], refs[-1]
        gather_into(whole, refs[:s], gathered, place_ref[1])
        blocks = basis_blocks(refs[s:], bases, k0, place_ref[2])
        for m in range(n):
            out[m][0] = (-galore_gain / width_root * dot_nt(blocks[m], whole[...])).astype(BF16)

    return call(
        body,
        (kc,),
        place,
        [(r, (1, 1, part, rank), lambda i, p: (0, i, 0, 0)) for r in flat]
        + basis_ins(bases, k0),
        [((kc, rows, width), BF16, (1, rows, width), lambda i, p: (i, 0, 0))] * n,
        [pltpu.VMEM((width, rank), BF16)],
    )


def place_delta(place, parts, before, k0, matrices):
    kc, rows, width = parts[0].shape
    n = len(parts)

    def body(place_ref, *refs):
        out = refs[-1]
        for m in range(n):
            at = pl.multiple_of(jnp.bitwise_xor(place_ref[0], m) * width, width)
            out[0, :, pl.ds(at, width)] = refs[m][0]

    ins = [(p, (1, rows, width), lambda i, p: (i, 0, 0)) for p in parts]
    aliases = {}
    if before is not None:
        ins.append((before, None, None))
        aliases = {n + 1: 0}
    shape = (matrices, rows, n * width)
    return call(
        body,
        (kc,),
        place,
        ins,
        [(shape, BF16, (1, rows, n * width), lambda i, p: (k0 + i, 0, 0))],
        [],
        aliases,
    )[0]


def gram_parts(place, groups):
    n = len(groups[0])
    rows, rank = groups[0][0].shape[1:]
    counts = [g[0].shape[0] for g in groups]
    total = sum(counts)
    part = rank // n
    flat = [p for g in groups for p in g]

    def body(place_ref, *refs):
        pieces, sub, out, whole = refs[: len(flat)], refs[len(flat)], refs[len(flat) + 1 : -1], refs[-1]
        at = 0
        for j, count in enumerate(counts):
            for i in range(count):
                acc = pieces[j * n][i]
                for m in range(1, n):
                    acc += pieces[j * n + m][i]
                sub[at] = acc
                high = split(acc)
                whole[at] = fine(dot_tn, high, high)
                at += 1
        for m in range(n):
            start = pl.multiple_of(jnp.bitwise_xor(place_ref[0], m) * part, part)
            for i in range(total):
                out[m][i] = whole[i, pl.ds(start, part), :]

    zero3 = lambda i, p: (0, 0, 0)
    res = call(
        body,
        (1,),
        place,
        [(p, p.shape, zero3) for p in flat],
        [((total, rows, rank), F32, (total, rows, rank), zero3)]
        + [((total, part, rank), F32, (total, part, rank), zero3)] * n,
        [pltpu.VMEM((total, rank, rank), F32)],
    )
    return res[0], res[1:]


def newton_schulz(place, pieces, sub):
    n = len(pieces)
    total, rows, rank = sub.shape
    part = rank // n

    def body(place_ref, *refs):
        p, s, out, whole = refs[:n], refs[n], refs[n + 1], refs[-1]
        for m in range(n):
            start = pl.multiple_of(jnp.bitwise_xor(place_ref[0], m) * part, part)
            for i in range(total):
                whole[i, pl.ds(start, part), :] = p[m][i]
        row = lax.broadcasted_iota(jnp.int32, (rank, rank), 0)
        col = lax.broadcasted_iota(jnp.int32, (rank, rank), 1)
        eye = jnp.where(row == col, 1.0, 0.0).astype(F32)
        iters, grams, prods = [], [], []
        for i in range(total):
            gram = whole[i]
            bound = jnp.max(jnp.sum(jnp.abs(gram), axis=1, keepdims=True), axis=0, keepdims=True) + 1e-06
            iters.append(s[i] / jnp.sqrt(bound))
            grams.append(gram / bound)
            prods.append(None)
        for turn in range(NS_ITERS):
            for i in range(total):
                factor = 1.5 * eye - 0.5 * grams[i]
                f = split(factor)
                prods[i] = factor if turn == 0 else fine(dot_nn, split(prods[i]), f)
                if turn + 1 < NS_ITERS:
                    half = fine(dot_nn, split(grams[i]), f)
                    grams[i] = fine(dot_nn, split(half), f)
        for i in range(total):
            res = fine(dot_nn, split(iters[i]), split(prods[i]))
            out[i] = (width_root * res).astype(BF16)

    zero3 = lambda i, p: (0, 0, 0)
    return call(
        body,
        (1,),
        place,
        [(p, p.shape, zero3) for p in pieces] + [(sub, sub.shape, zero3)],
        [((total, rows, rank), BF16, (total, rows, rank), zero3)],
        [pltpu.VMEM((total, rank, rank), F32)],
    )[0]


def after(x, *others):
    return lax.optimization_barrier((x, others))[0]


def per_device(shape, gradient, basis, moment_m, moment_v):
    tensors, sections, cores = shape["tensor"], shape["section"], shape["shard"]
    t, z, c = (lax.axis_index(a) for a in ("tensor", "section", "shard"))
    place = jnp.stack([t, z, c]).astype(jnp.int32)
    matrices = gradient.shape[0]
    split_cores = cores == 2
    n = len(CHUNKS)
    starts = [sum(CHUNKS[:j]) for j in range(n)]

    def swap(x, axis, m):
        return lax.ppermute(x, axis, [(i, i ^ m) for i in range(shape[axis])])

    token = ()

    def event(*values):
        nonlocal token, place
        token = values
        place = after(place, *values)

    def send(x, axis, m):
        return swap(after(x, *token), axis, m)

    def other_core(x):
        return lax.ppermute(after(x, *token), "shard", [(0, 1), (1, 0)])

    def send_all(cut):
        return [send(cut[m - 1], "tensor", m) for m in range(1, tensors)]

    grads, parts, sums, roughs, steps, cuts, subs, groups = ({} for _ in range(8))
    state = {"news": None, "delta": None}
    wide = sections != 4

    def cut(j):
        cuts[j] = outgoing(place, gradient, starts[j], CHUNKS[j], tensors)
        event(*cuts[j])

    def send_grads(j):
        grads[j] = send_all(cuts[j])

    def wait_grads(j):
        event(*grads[j])

    def low(j):
        parts[j] = low_partial(place, gradient, bases, grads[j], starts[j], sections)
        event(*parts[j])

    def sum_far(j):
        sums[j] = [parts[j][0]] + [None] * (sections - 1)
        if wide:
            sums[j][1:] = [send(x, "section", m + 1) for m, x in enumerate(parts[j][1:])]
        else:
            sums[j][2] = send(parts[j][3], "section", 1)
            sums[j].pop()

    def sum_near(j):
        if not wide:
            sums[j][1] = send(parts[j][1], "section", 1)

    def sum_two(j):
        if not wide:
            event(sums[j][2])
            both = parts[j][2].astype(F32) + sums[j][2].astype(F32)
            sums[j][2] = send(both.astype(BF16), "section", 2)

    def step(j):
        event(*sums[j])
        *low_out, m_new, v_new = update(
            place, sums[j], moment_m, moment_v, state["news"], starts[j], False
        )
        state["news"] = [m_new, v_new]
        roughs[j], steps[j] = [[[x]] + [None] * (sections - 1) for x in low_out]
        event(*low_out)

    def gather_two(held):
        if wide:
            held[1:] = [[send(held[0][0], "section", m)] for m in range(1, sections)]
        else:
            held[2] = [send(held[0][0], "section", 2)]

    def gather_near(held):
        if not wide:
            held[1] = [send(held[0][0], "section", 1)]

    def gather_far(held):
        if not wide:
            event(held[2][0])
            held[3] = [send(held[2][0], "section", 1)]

    def hop(x, pairs):
        return lax.ppermute(after(x, *token), "section", pairs)

    inwards, across, outwards = ((0, 1), (3, 2)), ((1, 2), (2, 1)), ((1, 0), (2, 3))

    def sum_in(j):
        sums[j] = {"own": parts[j][0]}
        if wide:
            sums[j]["all"] = [send(x, "section", m + 1) for m, x in enumerate(parts[j][1:])]
        else:
            sums[j]["end"] = hop(parts[j][3], inwards)

    def sum_in_two(j):
        if not wide:
            sums[j]["inner"] = hop(parts[j][2], inwards)

    def merged(x, y):
        return (x.astype(F32) + y.astype(F32)).astype(BF16)

    def sum_across(j):
        if not wide:
            event(sums[j]["end"])
            sums[j]["end"] = hop(merged(parts[j][2], sums[j]["end"]), across)

    def sum_across_two(j):
        if not wide:
            event(sums[j]["inner"])
            sums[j]["inner"] = hop(merged(parts[j][3], sums[j]["inner"]), across)

    def sum_out(j):
        if wide:
            sums[j] = [sums[j]["own"]] + sums[j]["all"]
        else:
            event(sums[j]["end"])
            last = send(merged(parts[j][1], sums[j]["end"]), "section", 1)
            sums[j] = [sums[j]["own"], sums[j]["inner"], last]

    def spread_across(held):
        if not wide:
            held[3] = [hop(held[0][0], across)]

    def spread_across_two(held):
        if not wide:
            event(held[1][0])
            held[2] = [hop(held[1][0], across)]

    def spread_out(held):
        if not wide:
            event(held[3][0])
            held[2].append(hop(held[3][0], outwards))

    def spread_out_two(held):
        if wide:
            gather_two(held)
        else:
            event(held[2][0])
            held[3].append(hop(held[2][0], outwards))

    def rough_across(j):
        spread_across(roughs[j])

    def rough_across_two(j):
        spread_across_two(roughs[j])

    def rough_out(j):
        spread_out(roughs[j])

    def rough_out_two(j):
        spread_out_two(roughs[j])

    def step_across(j):
        spread_across(steps[j])

    def step_across_two(j):
        spread_across_two(steps[j])

    def step_out(j):
        spread_out(steps[j])

    def step_out_two(j):
        spread_out_two(steps[j])

    def rough_two(j):
        gather_two(roughs[j])

    def rough_near(j):
        gather_near(roughs[j])

    def rough_far(j):
        gather_far(roughs[j])

    def step_two(j):
        gather_two(steps[j])

    def step_near(j):
        gather_near(steps[j])

    def step_far(j):
        gather_far(steps[j])

    def subspace(j):
        event(roughs[j])
        subs[j] = subspace_partial(place, gradient, grads[j], roughs[j], starts[j], split_cores)
        event(subs[j])

    def share(j):
        if split_cores:
            groups[j] = other_core(subs[j][CHUNKS[j] // 2 :])
        else:
            groups[j] = lax.psum(subs[j], "shard")

    def spread(j):
        event(groups[j])
        total = groups[j]
        if split_cores:
            total = total + subs[j][: CHUNKS[j] // 2]
        groups[j] = [total[:, 0]] + [send(total[:, m], "tensor", m) for m in range(1, tensors)]

    def wait_spread(j):
        event(*groups[j])

    def delta(j):
        event(steps[j])
        cuts[j] = delta_parts(place, bases, steps[j], starts[j])
        event(*cuts[j])

    def send_delta(j):
        cuts[j] = [cuts[j][0]] + send_all(cuts[j][1:])

    def put(j):
        event(*cuts[j])
        state["delta"] = place_delta(place, cuts[j], state["delta"], starts[j], matrices)
        event(state["delta"])

    def fetch():
        mine = basis
        if split_cores:
            mine = lax.dynamic_slice_in_dim(basis, c * (matrices // 2), matrices // 2, 0)
            event(mine)
        bases.extend([send(mine, "tensor", m)] for m in range(1, tensors))

    def hand_over():
        if split_cores:
            event(*[group[0] for group in bases[1:]])
            for group in bases[1:]:
                group.append(other_core(group[0]))

    def gram_kernel():
        state["sub"], state["gram"] = gram_parts(place, [groups[j] for j in range(n)])
        event(*state["gram"])

    def gram_send():
        cut = state["gram"]
        state["gram"] = [cut[0]] + send_all(cut[1:])

    def gram_sum():
        event(*state["gram"])
        state["gram"] = functools.reduce(jnp.add, state["gram"])
        state["reach"] = 1

    def gram_hop():
        state["hop"] = send(state["gram"], "section", state["reach"])
        state["reach"] *= 2

    def gram_add():
        event(state["hop"])
        state["gram"] = state["gram"] + state["hop"]

    def gram_gather():
        gram = state["gram"]
        state["gram"] = [gram] + [send(gram, "tensor", m) for m in range(1, tensors)]

    def newton():
        event(*state["gram"])
        state["done"] = newton_schulz(place, state["gram"], state["sub"])
        event(state["done"])

    def finish():
        done = state["done"]
        if split_cores:
            theirs = other_core(done)
            even = jnp.where(c == 0, done, theirs)
            odd = jnp.where(c == 0, theirs, done)
            done = jnp.stack([even, odd], 1).reshape(basis.shape)
        state["done"] = done

    bases = [[basis]]
    fetch()
    cut(0)
    hand_over()
    send_grads(0)
    cut(1)
    wait_grads(0)
    send_grads(1)
    low(0)
    sum_far(0)
    sum_near(0)
    sum_two(0)
    cut(2)
    step(0)
    step_two(0)
    rough_two(0)
    rough_near(0)
    wait_grads(1)
    send_grads(2)
    low(1)
    sum_far(1)
    sum_near(1)
    rough_far(0)
    sum_two(1)
    subspace(0)
    share(0)
    step_near(0)
    step(1)
    rough_two(1)
    rough_near(1)
    wait_grads(2)
    step_far(0)
    low(2)
    sum_far(2)
    sum_near(2)
    rough_far(1)
    sum_two(2)
    delta(0)
    spread(0)
    subspace(1)
    share(1)
    send_delta(0)
    step(2)
    rough_two(2)
    rough_near(2)
    rough_far(2)
    subspace(2)
    step_two(1)
    step_near(1)
    spread(1)
    put(0)
    share(2)
    step_far(1)
    step_two(2)
    step_near(2)
    spread(2)
    wait_spread(1)
    delta(1)
    send_delta(1)
    wait_spread(0)
    step_far(2)
    wait_spread(2)
    gram_kernel()
    gram_send()
    gram_sum()
    gram_hop()
    put(1)
    delta(2)
    gram_add()
    gram_hop()
    gram_add()
    gram_gather()
    newton()
    send_delta(2)
    finish()
    put(2)
    return (state["delta"], state["done"], *state["news"])


def solution(mesh):
    placed = (
        P(None, ("tensor", "section"), "shard"),
        P(None, ("tensor", "section"), None),
        P(None, ("shard", "tensor", "section"), None),
        P(None, ("shard", "tensor", "section"), None),
    )
    return jax.shard_map(
        functools.partial(per_device, dict(mesh.shape)),
        mesh=mesh,
        in_specs=placed,
        out_specs=placed,
        check_vma=False,
    )
```

```python
import functools
import math

import jax
import jax.numpy as jnp
from jax import lax
from jax.experimental import pallas as pl
from jax.experimental.pallas import tpu as pltpu
from jax.sharding import PartitionSpec as P

D = 2048
NS_ITERS = 4
CHUNKS = (2, 2, 2)
VMEM_LIMIT = 24 * 1024 * 1024

beta_one = 0.9
beta_two = 0.999
bias_one = 1.0 - 0.9**10
bias_two = 1.0 - 0.999**10
eps_adam = 1e-08
galore_gain = 4.0
width_root = math.sqrt(D)

F32 = jnp.float32
BF16 = jnp.bfloat16


def dot_tn(a, b):
    return lax.dot_general(a, b, (((0,), (0,)), ((), ())), preferred_element_type=F32)


def dot_nn(a, b):
    return lax.dot_general(a, b, (((1,), (0,)), ((), ())), preferred_element_type=F32)


def dot_nt(a, b):
    return lax.dot_general(a, b, (((1,), (1,)), ((), ())), preferred_element_type=F32)


def split(a):
    high = a.astype(BF16)
    return high, (a - high.astype(F32)).astype(BF16)


def fine(dot, a, b):
    (ah, al), (bh, bl) = a, b
    return dot(ah, bh) + (dot(ah, bl) + dot(al, bh))


def call(body, grid, prefetch, ins, outs, scratch, aliases=None, vmem=VMEM_LIMIT):
    return pl.pallas_call(
        body,
        grid_spec=pltpu.PrefetchScalarGridSpec(
            num_scalar_prefetch=1,
            grid=grid,
            in_specs=[
                pl.BlockSpec(memory_space=pl.ANY) if b is None else pl.BlockSpec(b, m)
                for _, b, m in ins
            ],
            out_specs=[pl.BlockSpec(b, m) for _, _, b, m in outs],
            scratch_shapes=scratch,
        ),
        out_shape=[jax.ShapeDtypeStruct(s, d) for s, d, _, _ in outs],
        input_output_aliases=aliases or {},
        compiler_params=pltpu.CompilerParams(vmem_limit_bytes=vmem),
        cost_estimate=pl.CostEstimate(flops=1, bytes_accessed=1, transcendentals=0),
    )(prefetch, *[a for a, _, _ in ins])


def outgoing(place, gradient, k0, kc, tensors):
    rows, columns = gradient.shape[1:]
    width = columns // tensors
    n = tensors - 1

    def body(place_ref, *refs):
        for m in range(n):
            refs[n + m][...] = refs[m][...]

    return call(
        body,
        (kc,),
        place,
        [
            (gradient, (1, rows, width), lambda i, p, m=m: (k0 + i, 0, jnp.bitwise_xor(p[0], m)))
            for m in range(1, tensors)
        ],
        [((kc, rows, width), BF16, (1, rows, width), lambda i, p: (i, 0, 0))] * n,
        [],
        vmem=60 * 1024 * 1024 if k0 == 0 else VMEM_LIMIT,
    )


def gradient_ins(gradient, got, k0, pick=lambda i, p: i):
    kc, rows, width = got[0].shape
    return [(gradient, (1, rows, width), lambda i, p: (k0 + pick(i, p), 0, p[0]))] + [
        (g, (1, rows, width), lambda i, p: (pick(i, p), 0, 0)) for g in got
    ]


def basis_ins(bases, k0):
    return [
        (a, (1,) + a.shape[1:], lambda i, p, n=a.shape[0]: (lax.rem(k0 + i, n), 0, 0))
        for group in bases
        for a in group
    ]


def basis_blocks(refs, bases, k0, core):
    refs = list(refs)
    blocks = []
    for group in bases:
        mine = refs.pop(0)[0]
        if len(group) == 2:
            owner = (k0 + pl.program_id(0)) // group[0].shape[0]
            mine = jnp.where(owner == core, mine, refs.pop(0)[0])
        blocks.append(mine)
    return blocks


def low_partial(place, gradient, bases, got, k0, sections):
    kc, rows, width = got[0].shape
    rank = bases[0][0].shape[2]
    part = width // sections
    n = len(bases)
    chosen = blocks_sent(sections)

    def body(place_ref, *refs):
        out, total = refs[-1 - len(chosen) : -1], refs[-1]
        blocks = basis_blocks(refs[n:], bases, k0, place_ref[2])
        acc = dot_tn(refs[0][0], blocks[0])
        for m in range(1, n):
            acc += dot_tn(refs[m][0], blocks[m])
        total[...] = acc
        z = place_ref[1]
        for j, block in enumerate(chosen):
            at = pl.multiple_of(block(z) * part, part)
            out[j][0] = total[pl.ds(at, part), :].astype(out[j].dtype)

    return call(
        body,
        (kc,),
        place,
        gradient_ins(gradient, got, k0) + basis_ins(bases, k0),
        [
            ((kc, part, rank), BF16 if j else F32, (1, part, rank), lambda i, p: (i, 0, 0))
            for j in range(len(chosen))
        ],
        [pltpu.VMEM((width, rank), F32)],
    )


def blocks_sent(sections):
    return [lambda z, m=m: jnp.bitwise_xor(z, m) for m in range(sections)]


def gather_into(whole, refs, gathered, z):
    refs = list(refs)
    part = refs[0].shape[-2]
    for j, group in enumerate(gathered):
        block = refs.pop(0)[0, 0]
        for _ in group[1:]:
            block = block + refs.pop(0)[0, 0]
        at = pl.multiple_of(jnp.bitwise_xor(z, j) * part, part)
        whole[pl.ds(at, part), :] = block


def update(place, terms, moment_m, moment_v, before, k0, joined):
    kc, part, rank = terms[0].shape
    n = len(terms)

    def body(place_ref, *refs):
        m_ref, v_ref = refs[n], refs[n + 1]
        *low_out, m_out, v_out = refs[-4 + joined :]
        total = refs[0][0]
        for j in range(1, n):
            total += refs[j][0].astype(F32)
        low_rank = total / width_root
        m_new = beta_one * m_ref[0] + (1.0 - beta_one) * low_rank
        v_new = beta_two * v_ref[0] + (1.0 - beta_two) * low_rank * low_rank
        step = m_new / bias_one / (jnp.sqrt(v_new / bias_two) + eps_adam)
        low_out[0][0, 0] = low_rank.astype(BF16)
        low_out[-1][int(joined), 0] = step.astype(BF16)
        m_out[0] = m_new
        v_out[0] = v_new

    here = lambda i, p: (k0 + i, 0, 0)
    block = (1, part, rank)
    ins = [(a, block, lambda i, p: (i, 0, 0)) for a in terms]
    ins += [(moment_m, block, here), (moment_v, block, here)]
    aliases = {}
    if before is not None:
        ins += [(b, None, None) for b in before]
        aliases = {n + 3: 2 - joined, n + 4: 3 - joined}
    return call(
        body,
        (kc,),
        place,
        ins,
        [
            (
                (1 + joined, kc, part, rank),
                BF16,
                (1 + joined, 1, part, rank),
                lambda i, p: (0, i, 0, 0),
            )
        ]
        * (2 - joined)
        + [
            (moment_m.shape, F32, block, here),
            (moment_v.shape, F32, block, here),
        ],
        [],
        aliases,
    )


def subspace_partial(place, gradient, got, gathered, k0, split_cores):
    kc, rows, width = got[0].shape
    flat = [r for group in gathered for r in group]
    part, rank = flat[0].shape[2:]
    n, s = len(got) + 1, len(flat)
    half = kc // 2

    def pick(i, p):
        if not split_cores:
            return i
        return jnp.where(i < half, 2 * i + p[2], 2 * (i - half) + 1 - p[2])

    def body(place_ref, *refs):
        out, whole = refs[-2:]
        gather_into(whole, refs[n : n + s], gathered, place_ref[1])
        for m in range(n):
            out[0, m] = dot_nn(refs[m][0], whole[...])

    return call(
        body,
        (kc,),
        place,
        gradient_ins(gradient, got, k0, pick)
        + [(r, (1, 1, part, rank), lambda i, p: (0, pick(i, p), 0, 0)) for r in flat],
        [((kc, n, rows, rank), F32, (1, n, rows, rank), lambda i, p: (i, 0, 0, 0))],
        [pltpu.VMEM((width, rank), BF16)],
    )[0]


def delta_parts(place, bases, gathered, k0):
    flat = [r for group in gathered for r in group]
    kc, part, rank = flat[0].shape[1:]
    rows = bases[0][0].shape[1]
    n, s = len(bases), len(flat)
    width = part * len(gathered)

    def body(place_ref, *refs):
        out, whole = refs[-1 - n : -1], refs[-1]
        gather_into(whole, refs[:s], gathered, place_ref[1])
        blocks = basis_blocks(refs[s:], bases, k0, place_ref[2])
        for m in range(n):
            out[m][0] = (-galore_gain / width_root * dot_nt(blocks[m], whole[...])).astype(BF16)

    return call(
        body,
        (kc,),
        place,
        [(r, (1, 1, part, rank), lambda i, p: (0, i, 0, 0)) for r in flat]
        + basis_ins(bases, k0),
        [((kc, rows, width), BF16, (1, rows, width), lambda i, p: (i, 0, 0))] * n,
        [pltpu.VMEM((width, rank), BF16)],
    )


def place_delta(place, parts, before, k0, matrices):
    kc, rows, width = parts[0].shape
    n = len(parts)

    def body(place_ref, *refs):
        out = refs[-1]
        for m in range(n):
            at = pl.multiple_of(jnp.bitwise_xor(place_ref[0], m) * width, width)
            out[0, :, pl.ds(at, width)] = refs[m][0]

    ins = [(p, (1, rows, width), lambda i, p: (i, 0, 0)) for p in parts]
    aliases = {}
    if before is not None:
        ins.append((before, None, None))
        aliases = {n + 1: 0}
    shape = (matrices, rows, n * width)
    return call(
        body,
        (kc,),
        place,
        ins,
        [(shape, BF16, (1, rows, n * width), lambda i, p: (k0 + i, 0, 0))],
        [],
        aliases,
    )[0]


def gram_parts(place, groups):
    n = len(groups[0])
    rows, rank = groups[0][0].shape[1:]
    counts = [g[0].shape[0] for g in groups]
    total = sum(counts)
    part = rank // n
    flat = [p for g in groups for p in g]

    def body(place_ref, *refs):
        pieces, sub, out, whole = refs[: len(flat)], refs[len(flat)], refs[len(flat) + 1 : -1], refs[-1]
        at = 0
        for j, count in enumerate(counts):
            for i in range(count):
                acc = pieces[j * n][i]
                for m in range(1, n):
                    acc += pieces[j * n + m][i]
                sub[at] = acc
                high = split(acc)
                whole[at] = fine(dot_tn, high, high)
                at += 1
        for m in range(n):
            start = pl.multiple_of(jnp.bitwise_xor(place_ref[0], m) * part, part)
            for i in range(total):
                out[m][i] = whole[i, pl.ds(start, part), :]

    zero3 = lambda i, p: (0, 0, 0)
    res = call(
        body,
        (1,),
        place,
        [(p, p.shape, zero3) for p in flat],
        [((total, rows, rank), F32, (total, rows, rank), zero3)]
        + [((total, part, rank), F32, (total, part, rank), zero3)] * n,
        [pltpu.VMEM((total, rank, rank), F32)],
    )
    return res[0], res[1:]


def newton_schulz(place, pieces, sub):
    n = len(pieces)
    total, rows, rank = sub.shape
    part = rank // n

    def body(place_ref, *refs):
        p, s, out, whole = refs[:n], refs[n], refs[n + 1], refs[-1]
        for m in range(n):
            start = pl.multiple_of(jnp.bitwise_xor(place_ref[0], m) * part, part)
            for i in range(total):
                whole[i, pl.ds(start, part), :] = p[m][i]
        row = lax.broadcasted_iota(jnp.int32, (rank, rank), 0)
        col = lax.broadcasted_iota(jnp.int32, (rank, rank), 1)
        eye = jnp.where(row == col, 1.0, 0.0).astype(F32)
        iters, grams, prods = [], [], []
        for i in range(total):
            gram = whole[i]
            bound = jnp.max(jnp.sum(jnp.abs(gram), axis=1, keepdims=True), axis=0, keepdims=True) + 1e-06
            iters.append(s[i] / jnp.sqrt(bound))
            grams.append(gram / bound)
            prods.append(None)
        for turn in range(NS_ITERS):
            for i in range(total):
                factor = 1.5 * eye - 0.5 * grams[i]
                f = split(factor)
                prods[i] = factor if turn == 0 else fine(dot_nn, split(prods[i]), f)
                if turn + 1 < NS_ITERS:
                    half = fine(dot_nn, split(grams[i]), f)
                    grams[i] = fine(dot_nn, split(half), f)
        for i in range(total):
            res = fine(dot_nn, split(iters[i]), split(prods[i]))
            out[i] = (width_root * res).astype(BF16)

    zero3 = lambda i, p: (0, 0, 0)
    return call(
        body,
        (1,),
        place,
        [(p, p.shape, zero3) for p in pieces] + [(sub, sub.shape, zero3)],
        [((total, rows, rank), BF16, (total, rows, rank), zero3)],
        [pltpu.VMEM((total, rank, rank), F32)],
    )[0]


def after(x, *others):
    return lax.optimization_barrier((x, others))[0]


def per_device(shape, gradient, basis, moment_m, moment_v):
    tensors, sections, cores = shape["tensor"], shape["section"], shape["shard"]
    t, z, c = (lax.axis_index(a) for a in ("tensor", "section", "shard"))
    place = jnp.stack([t, z, c]).astype(jnp.int32)
    matrices = gradient.shape[0]
    split_cores = cores == 2
    n = len(CHUNKS)
    starts = [sum(CHUNKS[:j]) for j in range(n)]

    def swap(x, axis, m):
        return lax.ppermute(x, axis, [(i, i ^ m) for i in range(shape[axis])])

    token = ()

    def event(*values):
        nonlocal token, place
        token = values
        place = after(place, *values)

    def send(x, axis, m):
        return swap(after(x, *token), axis, m)

    def other_core(x):
        return lax.ppermute(after(x, *token), "shard", [(0, 1), (1, 0)])

    def send_all(cut):
        return [send(cut[m - 1], "tensor", m) for m in range(1, tensors)]

    grads, parts, sums, roughs, steps, cuts, subs, groups = ({} for _ in range(8))
    state = {"news": None, "delta": None}
    wide = sections != 4

    def cut(j):
        cuts[j] = outgoing(place, gradient, starts[j], CHUNKS[j], tensors)
        event(*cuts[j])

    def send_grads(j):
        grads[j] = send_all(cuts[j])

    def wait_grads(j):
        event(*grads[j])

    def low(j):
        parts[j] = low_partial(place, gradient, bases, grads[j], starts[j], sections)
        event(*parts[j])

    def sum_far(j):
        sums[j] = [parts[j][0]] + [None] * (sections - 1)
        if wide:
            sums[j][1:] = [send(x, "section", m + 1) for m, x in enumerate(parts[j][1:])]
        else:
            sums[j][2] = send(parts[j][3], "section", 1)
            sums[j].pop()

    def sum_near(j):
        if not wide:
            sums[j][1] = send(parts[j][1], "section", 1)

    def sum_two(j):
        if not wide:
            event(sums[j][2])
            both = parts[j][2].astype(F32) + sums[j][2].astype(F32)
            sums[j][2] = send(both.astype(BF16), "section", 2)

    def step(j):
        event(*sums[j])
        *low_out, m_new, v_new = update(
            place, sums[j], moment_m, moment_v, state["news"], starts[j], False
        )
        state["news"] = [m_new, v_new]
        roughs[j], steps[j] = [[[x]] + [None] * (sections - 1) for x in low_out]
        event(*low_out)

    def gather_two(held):
        if wide:
            held[1:] = [[send(held[0][0], "section", m)] for m in range(1, sections)]
        else:
            held[2] = [send(held[0][0], "section", 2)]

    def gather_near(held):
        if not wide:
            held[1] = [send(held[0][0], "section", 1)]

    def gather_far(held):
        if not wide:
            event(held[2][0])
            held[3] = [send(held[2][0], "section", 1)]

    def hop(x, pairs):
        return lax.ppermute(after(x, *token), "section", pairs)

    inwards, across, outwards = ((0, 1), (3, 2)), ((1, 2), (2, 1)), ((1, 0), (2, 3))

    def sum_in(j):
        sums[j] = {"own": parts[j][0]}
        if wide:
            sums[j]["all"] = [send(x, "section", m + 1) for m, x in enumerate(parts[j][1:])]
        else:
            sums[j]["end"] = hop(parts[j][3], inwards)

    def sum_in_two(j):
        if not wide:
            sums[j]["inner"] = hop(parts[j][2], inwards)

    def merged(x, y):
        return (x.astype(F32) + y.astype(F32)).astype(BF16)

    def sum_across(j):
        if not wide:
            event(sums[j]["end"])
            sums[j]["end"] = hop(merged(parts[j][2], sums[j]["end"]), across)

    def sum_across_two(j):
        if not wide:
            event(sums[j]["inner"])
            sums[j]["inner"] = hop(merged(parts[j][3], sums[j]["inner"]), across)

    def sum_out(j):
        if wide:
            sums[j] = [sums[j]["own"]] + sums[j]["all"]
        else:
            event(sums[j]["end"])
            last = send(merged(parts[j][1], sums[j]["end"]), "section", 1)
            sums[j] = [sums[j]["own"], sums[j]["inner"], last]

    def spread_across(held):
        if not wide:
            held[3] = [hop(held[0][0], across)]

    def spread_across_two(held):
        if not wide:
            event(held[1][0])
            held[2] = [hop(held[1][0], across)]

    def spread_out(held):
        if not wide:
            event(held[3][0])
            held[2].append(hop(held[3][0], outwards))

    def spread_out_two(held):
        if wide:
            gather_two(held)
        else:
            event(held[2][0])
            held[3].append(hop(held[2][0], outwards))

    def rough_across(j):
        spread_across(roughs[j])

    def rough_across_two(j):
        spread_across_two(roughs[j])

    def rough_out(j):
        spread_out(roughs[j])

    def rough_out_two(j):
        spread_out_two(roughs[j])

    def step_across(j):
        spread_across(steps[j])

    def step_across_two(j):
        spread_across_two(steps[j])

    def step_out(j):
        spread_out(steps[j])

    def step_out_two(j):
        spread_out_two(steps[j])

    def rough_two(j):
        gather_two(roughs[j])

    def rough_near(j):
        gather_near(roughs[j])

    def rough_far(j):
        gather_far(roughs[j])

    def step_two(j):
        gather_two(steps[j])

    def step_near(j):
        gather_near(steps[j])

    def step_far(j):
        gather_far(steps[j])

    def subspace(j):
        event(roughs[j])
        subs[j] = subspace_partial(place, gradient, grads[j], roughs[j], starts[j], split_cores)
        event(subs[j])

    def share(j):
        if split_cores:
            groups[j] = other_core(subs[j][CHUNKS[j] // 2 :])
        else:
            groups[j] = lax.psum(subs[j], "shard")

    def spread(j):
        event(groups[j])
        total = groups[j]
        if split_cores:
            total = total + subs[j][: CHUNKS[j] // 2]
        groups[j] = [total[:, 0]] + [send(total[:, m], "tensor", m) for m in range(1, tensors)]

    def wait_spread(j):
        event(*groups[j])

    def delta(j):
        event(steps[j])
        cuts[j] = delta_parts(place, bases, steps[j], starts[j])
        event(*cuts[j])

    def send_delta(j):
        cuts[j] = [cuts[j][0]] + send_all(cuts[j][1:])

    def put(j):
        event(*cuts[j])
        state["delta"] = place_delta(place, cuts[j], state["delta"], starts[j], matrices)
        event(state["delta"])

    def fetch():
        mine = basis
        if split_cores:
            mine = lax.dynamic_slice_in_dim(basis, c * (matrices // 2), matrices // 2, 0)
            event(mine)
        bases.extend([send(mine, "tensor", m)] for m in range(1, tensors))

    def hand_over():
        if split_cores:
            event(*[group[0] for group in bases[1:]])
            for group in bases[1:]:
                group.append(other_core(group[0]))

    def gram_kernel():
        state["sub"], state["gram"] = gram_parts(place, [groups[j] for j in range(n)])
        event(*state["gram"])

    def gram_send():
        cut = state["gram"]
        state["gram"] = [cut[0]] + send_all(cut[1:])

    def gram_sum():
        event(*state["gram"])
        state["gram"] = functools.reduce(jnp.add, state["gram"])
        state["reach"] = 1

    def gram_hop():
        state["hop"] = send(state["gram"], "section", state["reach"])
        state["reach"] *= 2

    def gram_add():
        event(state["hop"])
        state["gram"] = state["gram"] + state["hop"]

    def gram_gather():
        gram = state["gram"]
        state["gram"] = [gram] + [send(gram, "tensor", m) for m in range(1, tensors)]

    def newton():
        event(*state["gram"])
        state["done"] = newton_schulz(place, state["gram"], state["sub"])
        event(state["done"])

    def finish():
        done = state["done"]
        if split_cores:
            theirs = other_core(done)
            even = jnp.where(c == 0, done, theirs)
            odd = jnp.where(c == 0, theirs, done)
            done = jnp.stack([even, odd], 1).reshape(basis.shape)
        state["done"] = done

    bases = [[basis]]
    fetch()
    cut(0)
    hand_over()
    send_grads(0)
    cut(1)
    wait_grads(0)
    send_grads(1)
    low(0)
    sum_far(0)
    sum_near(0)
    sum_two(0)
    cut(2)
    step(0)
    rough_two(0)
    send_grads(2)
    step_two(0)
    wait_grads(1)
    rough_near(0)
    low(1)
    sum_far(1)
    sum_near(1)
    rough_far(0)
    sum_two(1)
    subspace(0)
    share(0)
    step_near(0)
    step(1)
    rough_across(1)
    wait_grads(2)
    step_far(0)
    rough_near(1)
    low(2)
    sum_far(2)
    sum_near(2)
    rough_across_two(1)
    sum_two(2)
    delta(0)
    send_delta(0)
    rough_out(1)
    step(2)
    rough_out_two(1)
    rough_two(2)
    subspace(1)
    rough_near(2)
    rough_far(2)
    spread(0)
    share(1)
    subspace(2)
    step_two(1)
    put(0)
    share(2)
    step_far(1)
    spread(1)
    step_near(1)
    step_two(2)
    step_near(2)
    spread(2)
    wait_spread(1)
    delta(1)
    send_delta(1)
    wait_spread(0)
    step_far(2)
    wait_spread(2)
    gram_kernel()
    gram_send()
    gram_sum()
    gram_hop()
    put(1)
    delta(2)
    gram_add()
    gram_hop()
    gram_add()
    gram_gather()
    newton()
    send_delta(2)
    finish()
    put(2)
    return (state["delta"], state["done"], *state["news"])


def solution(mesh):
    placed = (
        P(None, ("tensor", "section"), "shard"),
        P(None, ("tensor", "section"), None),
        P(None, ("shard", "tensor", "section"), None),
        P(None, ("shard", "tensor", "section"), None),
    )
    return jax.shard_map(
        functools.partial(per_device, dict(mesh.shape)),
        mesh=mesh,
        in_specs=placed,
        out_specs=placed,
        check_vma=False,
    )
```

```python
import functools
import math

import jax
import jax.numpy as jnp
from jax import lax
from jax.experimental import pallas as pl
from jax.experimental.pallas import tpu as pltpu
from jax.sharding import PartitionSpec as P

D = 2048
NS_ITERS = 4
CHUNKS = (2, 2, 2)
VMEM_LIMIT = 24 * 1024 * 1024

beta_one = 0.9
beta_two = 0.999
bias_one = 1.0 - 0.9**10
bias_two = 1.0 - 0.999**10
eps_adam = 1e-08
galore_gain = 4.0
width_root = math.sqrt(D)

F32 = jnp.float32
BF16 = jnp.bfloat16


def dot_tn(a, b):
    return lax.dot_general(a, b, (((0,), (0,)), ((), ())), preferred_element_type=F32)


def dot_nn(a, b):
    return lax.dot_general(a, b, (((1,), (0,)), ((), ())), preferred_element_type=F32)


def dot_nt(a, b):
    return lax.dot_general(a, b, (((1,), (1,)), ((), ())), preferred_element_type=F32)


def split(a):
    high = a.astype(BF16)
    return high, (a - high.astype(F32)).astype(BF16)


def fine(dot, a, b):
    (ah, al), (bh, bl) = a, b
    return dot(ah, bh) + (dot(ah, bl) + dot(al, bh))


def call(body, grid, prefetch, ins, outs, scratch, aliases=None, vmem=VMEM_LIMIT):
    return pl.pallas_call(
        body,
        grid_spec=pltpu.PrefetchScalarGridSpec(
            num_scalar_prefetch=1,
            grid=grid,
            in_specs=[
                pl.BlockSpec(memory_space=pl.ANY) if b is None else pl.BlockSpec(b, m)
                for _, b, m in ins
            ],
            out_specs=[pl.BlockSpec(b, m) for _, _, b, m in outs],
            scratch_shapes=scratch,
        ),
        out_shape=[jax.ShapeDtypeStruct(s, d) for s, d, _, _ in outs],
        input_output_aliases=aliases or {},
        compiler_params=pltpu.CompilerParams(vmem_limit_bytes=vmem),
        cost_estimate=pl.CostEstimate(flops=1, bytes_accessed=1, transcendentals=0),
    )(prefetch, *[a for a, _, _ in ins])


def outgoing(place, gradient, k0, kc, tensors):
    rows, columns = gradient.shape[1:]
    width = columns // tensors
    n = tensors - 1

    def body(place_ref, *refs):
        for m in range(n):
            refs[n + m][...] = refs[m][...]

    return call(
        body,
        (kc,),
        place,
        [
            (gradient, (1, rows, width), lambda i, p, m=m: (k0 + i, 0, jnp.bitwise_xor(p[0], m)))
            for m in range(1, tensors)
        ],
        [((kc, rows, width), BF16, (1, rows, width), lambda i, p: (i, 0, 0))] * n,
        [],
        vmem=60 * 1024 * 1024 if k0 == 0 else VMEM_LIMIT,
    )


def gradient_ins(gradient, got, k0, pick=lambda i, p: i):
    kc, rows, width = got[0].shape
    return [(gradient, (1, rows, width), lambda i, p: (k0 + pick(i, p), 0, p[0]))] + [
        (g, (1, rows, width), lambda i, p: (pick(i, p), 0, 0)) for g in got
    ]


def basis_ins(bases, k0):
    return [
        (a, (1,) + a.shape[1:], lambda i, p, n=a.shape[0]: (lax.rem(k0 + i, n), 0, 0))
        for group in bases
        for a in group
    ]


def basis_blocks(refs, bases, k0, core):
    refs = list(refs)
    blocks = []
    for group in bases:
        mine = refs.pop(0)[0]
        if len(group) == 2:
            owner = (k0 + pl.program_id(0)) // group[0].shape[0]
            mine = jnp.where(owner == core, mine, refs.pop(0)[0])
        blocks.append(mine)
    return blocks


def low_partial(place, gradient, bases, got, k0, sections):
    kc, rows, width = got[0].shape
    rank = bases[0][0].shape[2]
    part = width // sections
    n = len(bases)
    chosen = blocks_sent(sections)

    def body(place_ref, *refs):
        out, total = refs[-1 - len(chosen) : -1], refs[-1]
        blocks = basis_blocks(refs[n:], bases, k0, place_ref[2])
        acc = dot_tn(refs[0][0], blocks[0])
        for m in range(1, n):
            acc += dot_tn(refs[m][0], blocks[m])
        total[...] = acc
        z = place_ref[1]
        for j, block in enumerate(chosen):
            at = pl.multiple_of(block(z) * part, part)
            out[j][0] = total[pl.ds(at, part), :].astype(out[j].dtype)

    return call(
        body,
        (kc,),
        place,
        gradient_ins(gradient, got, k0) + basis_ins(bases, k0),
        [
            ((kc, part, rank), BF16 if j else F32, (1, part, rank), lambda i, p: (i, 0, 0))
            for j in range(len(chosen))
        ],
        [pltpu.VMEM((width, rank), F32)],
    )


def blocks_sent(sections):
    return [lambda z, m=m: jnp.bitwise_xor(z, m) for m in range(sections)]


def gather_into(whole, refs, gathered, z):
    refs = list(refs)
    part = refs[0].shape[-2]
    for j, group in enumerate(gathered):
        block = refs.pop(0)[0, 0]
        for _ in group[1:]:
            block = block + refs.pop(0)[0, 0]
        at = pl.multiple_of(jnp.bitwise_xor(z, j) * part, part)
        whole[pl.ds(at, part), :] = block


def update(place, terms, moment_m, moment_v, before, k0, joined):
    kc, part, rank = terms[0].shape
    n = len(terms)

    def body(place_ref, *refs):
        m_ref, v_ref = refs[n], refs[n + 1]
        *low_out, m_out, v_out = refs[-4 + joined :]
        total = refs[0][0]
        for j in range(1, n):
            total += refs[j][0].astype(F32)
        low_rank = total / width_root
        m_new = beta_one * m_ref[0] + (1.0 - beta_one) * low_rank
        v_new = beta_two * v_ref[0] + (1.0 - beta_two) * low_rank * low_rank
        step = m_new / bias_one / (jnp.sqrt(v_new / bias_two) + eps_adam)
        low_out[0][0, 0] = low_rank.astype(BF16)
        low_out[-1][int(joined), 0] = step.astype(BF16)
        m_out[0] = m_new
        v_out[0] = v_new

    here = lambda i, p: (k0 + i, 0, 0)
    block = (1, part, rank)
    ins = [(a, block, lambda i, p: (i, 0, 0)) for a in terms]
    ins += [(moment_m, block, here), (moment_v, block, here)]
    aliases = {}
    if before is not None:
        ins += [(b, None, None) for b in before]
        aliases = {n + 3: 2 - joined, n + 4: 3 - joined}
    return call(
        body,
        (kc,),
        place,
        ins,
        [
            (
                (1 + joined, kc, part, rank),
                BF16,
                (1 + joined, 1, part, rank),
                lambda i, p: (0, i, 0, 0),
            )
        ]
        * (2 - joined)
        + [
            (moment_m.shape, F32, block, here),
            (moment_v.shape, F32, block, here),
        ],
        [],
        aliases,
    )


def subspace_partial(place, gradient, got, gathered, k0, split_cores):
    kc, rows, width = got[0].shape
    flat = [r for group in gathered for r in group]
    part, rank = flat[0].shape[2:]
    n, s = len(got) + 1, len(flat)
    half = kc // 2

    def pick(i, p):
        if not split_cores:
            return i
        return jnp.where(i < half, 2 * i + p[2], 2 * (i - half) + 1 - p[2])

    def body(place_ref, *refs):
        out, whole = refs[-2:]
        gather_into(whole, refs[n : n + s], gathered, place_ref[1])
        for m in range(n):
            out[0, m] = dot_nn(refs[m][0], whole[...])

    return call(
        body,
        (kc,),
        place,
        gradient_ins(gradient, got, k0, pick)
        + [(r, (1, 1, part, rank), lambda i, p: (0, pick(i, p), 0, 0)) for r in flat],
        [((kc, n, rows, rank), F32, (1, n, rows, rank), lambda i, p: (i, 0, 0, 0))],
        [pltpu.VMEM((width, rank), BF16)],
    )[0]


def delta_parts(place, bases, gathered, k0):
    flat = [r for group in gathered for r in group]
    kc, part, rank = flat[0].shape[1:]
    rows = bases[0][0].shape[1]
    n, s = len(bases), len(flat)
    width = part * len(gathered)

    def body(place_ref, *refs):
        out, whole = refs[-1 - n : -1], refs[-1]
        gather_into(whole, refs[:s], gathered, place_ref[1])
        blocks = basis_blocks(refs[s:], bases, k0, place_ref[2])
        for m in range(n):
            out[m][0] = (-galore_gain / width_root * dot_nt(blocks[m], whole[...])).astype(BF16)

    return call(
        body,
        (kc,),
        place,
        [(r, (1, 1, part, rank), lambda i, p: (0, i, 0, 0)) for r in flat]
        + basis_ins(bases, k0),
        [((kc, rows, width), BF16, (1, rows, width), lambda i, p: (i, 0, 0))] * n,
        [pltpu.VMEM((width, rank), BF16)],
    )


def place_delta(place, parts, before, k0, matrices):
    kc, rows, width = parts[0].shape
    n = len(parts)

    def body(place_ref, *refs):
        out = refs[-1]
        for m in range(n):
            at = pl.multiple_of(jnp.bitwise_xor(place_ref[0], m) * width, width)
            out[0, :, pl.ds(at, width)] = refs[m][0]

    ins = [(p, (1, rows, width), lambda i, p: (i, 0, 0)) for p in parts]
    aliases = {}
    if before is not None:
        ins.append((before, None, None))
        aliases = {n + 1: 0}
    shape = (matrices, rows, n * width)
    return call(
        body,
        (kc,),
        place,
        ins,
        [(shape, BF16, (1, rows, n * width), lambda i, p: (k0 + i, 0, 0))],
        [],
        aliases,
    )[0]


def gram_parts(place, groups):
    n = len(groups[0])
    rows, rank = groups[0][0].shape[1:]
    counts = [g[0].shape[0] for g in groups]
    total = sum(counts)
    part = rank // n
    flat = [p for g in groups for p in g]

    def body(place_ref, *refs):
        pieces, sub, out, whole = refs[: len(flat)], refs[len(flat)], refs[len(flat) + 1 : -1], refs[-1]
        at = 0
        for j, count in enumerate(counts):
            for i in range(count):
                acc = pieces[j * n][i]
                for m in range(1, n):
                    acc += pieces[j * n + m][i]
                sub[at] = acc
                high = split(acc)
                whole[at] = fine(dot_tn, high, high)
                at += 1
        for m in range(n):
            start = pl.multiple_of(jnp.bitwise_xor(place_ref[0], m) * part, part)
            for i in range(total):
                out[m][i] = whole[i, pl.ds(start, part), :]

    zero3 = lambda i, p: (0, 0, 0)
    res = call(
        body,
        (1,),
        place,
        [(p, p.shape, zero3) for p in flat],
        [((total, rows, rank), F32, (total, rows, rank), zero3)]
        + [((total, part, rank), F32, (total, part, rank), zero3)] * n,
        [pltpu.VMEM((total, rank, rank), F32)],
    )
    return res[0], res[1:]


def newton_schulz(place, pieces, sub):
    n = len(pieces)
    total, rows, rank = sub.shape
    part = rank // n

    def body(place_ref, *refs):
        p, s, out, whole = refs[:n], refs[n], refs[n + 1], refs[-1]
        for m in range(n):
            start = pl.multiple_of(jnp.bitwise_xor(place_ref[0], m) * part, part)
            for i in range(total):
                whole[i, pl.ds(start, part), :] = p[m][i]
        row = lax.broadcasted_iota(jnp.int32, (rank, rank), 0)
        col = lax.broadcasted_iota(jnp.int32, (rank, rank), 1)
        eye = jnp.where(row == col, 1.0, 0.0).astype(F32)
        iters, grams, prods = [], [], []
        for i in range(total):
            gram = whole[i]
            bound = jnp.max(jnp.sum(jnp.abs(gram), axis=1, keepdims=True), axis=0, keepdims=True) + 1e-06
            iters.append(s[i] / jnp.sqrt(bound))
            grams.append(gram / bound)
            prods.append(None)
        for turn in range(NS_ITERS):
            for i in range(total):
                factor = 1.5 * eye - 0.5 * grams[i]
                f = split(factor)
                prods[i] = factor if turn == 0 else fine(dot_nn, split(prods[i]), f)
                if turn + 1 < NS_ITERS:
                    half = fine(dot_nn, split(grams[i]), f)
                    grams[i] = fine(dot_nn, split(half), f)
        for i in range(total):
            res = fine(dot_nn, split(iters[i]), split(prods[i]))
            out[i] = (width_root * res).astype(BF16)

    zero3 = lambda i, p: (0, 0, 0)
    return call(
        body,
        (1,),
        place,
        [(p, p.shape, zero3) for p in pieces] + [(sub, sub.shape, zero3)],
        [((total, rows, rank), BF16, (total, rows, rank), zero3)],
        [pltpu.VMEM((total, rank, rank), F32)],
    )[0]


def after(x, *others):
    return lax.optimization_barrier((x, others))[0]


def per_device(shape, gradient, basis, moment_m, moment_v):
    tensors, sections, cores = shape["tensor"], shape["section"], shape["shard"]
    t, z, c = (lax.axis_index(a) for a in ("tensor", "section", "shard"))
    place = jnp.stack([t, z, c]).astype(jnp.int32)
    matrices = gradient.shape[0]
    split_cores = cores == 2
    n = len(CHUNKS)
    starts = [sum(CHUNKS[:j]) for j in range(n)]

    def swap(x, axis, m):
        return lax.ppermute(x, axis, [(i, i ^ m) for i in range(shape[axis])])

    token = ()

    def event(*values):
        nonlocal token, place
        token = values
        place = after(place, *values)

    def send(x, axis, m):
        return swap(after(x, *token), axis, m)

    def other_core(x):
        return lax.ppermute(after(x, *token), "shard", [(0, 1), (1, 0)])

    def send_all(cut):
        return [send(cut[m - 1], "tensor", m) for m in range(1, tensors)]

    grads, parts, sums, roughs, steps, cuts, subs, groups = ({} for _ in range(8))
    state = {"news": None, "delta": None}
    wide = sections != 4

    def cut(j):
        cuts[j] = outgoing(place, gradient, starts[j], CHUNKS[j], tensors)
        event(*cuts[j])

    def send_grads(j):
        grads[j] = send_all(cuts[j])

    def wait_grads(j):
        event(*grads[j])

    def low(j):
        parts[j] = low_partial(place, gradient, bases, grads[j], starts[j], sections)
        event(*parts[j])

    def sum_far(j):
        sums[j] = [parts[j][0]] + [None] * (sections - 1)
        if wide:
            sums[j][1:] = [send(x, "section", m + 1) for m, x in enumerate(parts[j][1:])]
        else:
            sums[j][2] = send(parts[j][3], "section", 1)
            sums[j].pop()

    def sum_near(j):
        if not wide:
            sums[j][1] = send(parts[j][1], "section", 1)

    def sum_two(j):
        if not wide:
            event(sums[j][2])
            both = parts[j][2].astype(F32) + sums[j][2].astype(F32)
            sums[j][2] = send(both.astype(BF16), "section", 2)

    def step(j):
        event(*sums[j])
        *low_out, m_new, v_new = update(
            place, sums[j], moment_m, moment_v, state["news"], starts[j], False
        )
        state["news"] = [m_new, v_new]
        roughs[j], steps[j] = [[[x]] + [None] * (sections - 1) for x in low_out]
        event(*low_out)

    def gather_two(held):
        if wide:
            held[1:] = [[send(held[0][0], "section", m)] for m in range(1, sections)]
        else:
            held[2] = [send(held[0][0], "section", 2)]

    def gather_near(held):
        if not wide:
            held[1] = [send(held[0][0], "section", 1)]

    def gather_far(held):
        if not wide:
            event(held[2][0])
            held[3] = [send(held[2][0], "section", 1)]

    def hop(x, pairs):
        return lax.ppermute(after(x, *token), "section", pairs)

    inwards, across, outwards = ((0, 1), (3, 2)), ((1, 2), (2, 1)), ((1, 0), (2, 3))

    def sum_in(j):
        sums[j] = {"own": parts[j][0]}
        if wide:
            sums[j]["all"] = [send(x, "section", m + 1) for m, x in enumerate(parts[j][1:])]
        else:
            sums[j]["end"] = hop(parts[j][3], inwards)

    def sum_in_two(j):
        if not wide:
            sums[j]["inner"] = hop(parts[j][2], inwards)

    def merged(x, y):
        return (x.astype(F32) + y.astype(F32)).astype(BF16)

    def sum_across(j):
        if not wide:
            event(sums[j]["end"])
            sums[j]["end"] = hop(merged(parts[j][2], sums[j]["end"]), across)

    def sum_across_two(j):
        if not wide:
            event(sums[j]["inner"])
            sums[j]["inner"] = hop(merged(parts[j][3], sums[j]["inner"]), across)

    def sum_out(j):
        if wide:
            sums[j] = [sums[j]["own"]] + sums[j]["all"]
        else:
            event(sums[j]["end"])
            last = send(merged(parts[j][1], sums[j]["end"]), "section", 1)
            sums[j] = [sums[j]["own"], sums[j]["inner"], last]

    def spread_across(held):
        if not wide:
            held[3] = [hop(held[0][0], across)]

    def spread_across_two(held):
        if not wide:
            event(held[1][0])
            held[2] = [hop(held[1][0], across)]

    def spread_out(held):
        if not wide:
            event(held[3][0])
            held[2].append(hop(held[3][0], outwards))

    def spread_out_two(held):
        if wide:
            gather_two(held)
        else:
            event(held[2][0])
            held[3].append(hop(held[2][0], outwards))

    def rough_across(j):
        spread_across(roughs[j])

    def rough_across_two(j):
        spread_across_two(roughs[j])

    def rough_out(j):
        spread_out(roughs[j])

    def rough_out_two(j):
        spread_out_two(roughs[j])

    def step_across(j):
        spread_across(steps[j])

    def step_across_two(j):
        spread_across_two(steps[j])

    def step_out(j):
        spread_out(steps[j])

    def step_out_two(j):
        spread_out_two(steps[j])

    def rough_two(j):
        gather_two(roughs[j])

    def rough_near(j):
        gather_near(roughs[j])

    def rough_far(j):
        gather_far(roughs[j])

    def step_two(j):
        gather_two(steps[j])

    def step_near(j):
        gather_near(steps[j])

    def step_far(j):
        gather_far(steps[j])

    def subspace(j):
        event(roughs[j])
        subs[j] = subspace_partial(place, gradient, grads[j], roughs[j], starts[j], split_cores)
        event(subs[j])

    def share(j):
        if split_cores:
            groups[j] = other_core(subs[j][CHUNKS[j] // 2 :])
        else:
            groups[j] = lax.psum(subs[j], "shard")

    def spread(j):
        event(groups[j])
        total = groups[j]
        if split_cores:
            total = total + subs[j][: CHUNKS[j] // 2]
        groups[j] = [total[:, 0]] + [send(total[:, m], "tensor", m) for m in range(1, tensors)]

    def wait_spread(j):
        event(*groups[j])

    def delta(j):
        event(steps[j])
        cuts[j] = delta_parts(place, bases, steps[j], starts[j])
        event(*cuts[j])

    def send_delta(j):
        cuts[j] = [cuts[j][0]] + send_all(cuts[j][1:])

    def put(j):
        event(*cuts[j])
        state["delta"] = place_delta(place, cuts[j], state["delta"], starts[j], matrices)
        event(state["delta"])

    def fetch():
        mine = basis
        if split_cores:
            mine = lax.dynamic_slice_in_dim(basis, c * (matrices // 2), matrices // 2, 0)
            event(mine)
        bases.extend([send(mine, "tensor", m)] for m in range(1, tensors))

    def hand_over():
        if split_cores:
            event(*[group[0] for group in bases[1:]])
            for group in bases[1:]:
                group.append(other_core(group[0]))

    def gram_kernel():
        state["sub"], state["gram"] = gram_parts(place, [groups[j] for j in range(n)])
        event(*state["gram"])

    def gram_send():
        cut = state["gram"]
        state["gram"] = [cut[0]] + send_all(cut[1:])

    def gram_sum():
        event(*state["gram"])
        state["gram"] = functools.reduce(jnp.add, state["gram"])
        state["reach"] = 1

    def gram_hop():
        state["hop"] = send(state["gram"], "section", state["reach"])
        state["reach"] *= 2

    def gram_add():
        event(state["hop"])
        state["gram"] = state["gram"] + state["hop"]

    def gram_gather():
        gram = state["gram"]
        state["gram"] = [gram] + [send(gram, "tensor", m) for m in range(1, tensors)]

    def newton():
        event(*state["gram"])
        state["done"] = newton_schulz(place, state["gram"], state["sub"])
        event(state["done"])

    def finish():
        done = state["done"]
        if split_cores:
            theirs = other_core(done)
            even = jnp.where(c == 0, done, theirs)
            odd = jnp.where(c == 0, theirs, done)
            done = jnp.stack([even, odd], 1).reshape(basis.shape)
        state["done"] = done

    bases = [[basis]]
    fetch()
    cut(0)
    hand_over()
    send_grads(0)
    cut(1)
    wait_grads(0)
    send_grads(1)
    low(0)
    sum_far(0)
    sum_near(0)
    sum_two(0)
    cut(2)
    step(0)
    rough_two(0)
    send_grads(2)
    wait_grads(1)
    rough_near(0)
    low(1)
    step_two(0)
    sum_far(1)
    rough_far(0)
    sum_near(1)
    sum_two(1)
    subspace(0)
    share(0)
    step_near(0)
    step(1)
    wait_grads(2)
    step_far(0)
    rough_across(1)
    rough_near(1)
    low(2)
    sum_far(2)
    sum_near(2)
    rough_across_two(1)
    sum_two(2)
    delta(0)
    send_delta(0)
    rough_out(1)
    step(2)
    step_near(1)
    rough_out_two(1)
    rough_two(2)
    step_two(1)
    rough_far(2)
    spread(0)
    rough_near(2)
    subspace(1)
    share(1)
    subspace(2)
    put(0)
    share(2)
    step_far(1)
    spread(1)
    step_two(2)
    step_near(2)
    spread(2)
    wait_spread(1)
    delta(1)
    wait_spread(0)
    send_delta(1)
    wait_spread(2)
    gram_kernel()
    gram_send()
    step_far(2)
    gram_sum()
    gram_hop()
    put(1)
    gram_add()
    gram_hop()
    gram_add()
    gram_gather()
    delta(2)
    newton()
    send_delta(2)
    finish()
    put(2)
    return (state["delta"], state["done"], *state["news"])


def solution(mesh):
    placed = (
        P(None, ("tensor", "section"), "shard"),
        P(None, ("tensor", "section"), None),
        P(None, ("shard", "tensor", "section"), None),
        P(None, ("shard", "tensor", "section"), None),
    )
    return jax.shard_map(
        functools.partial(per_device, dict(mesh.shape)),
        mesh=mesh,
        in_specs=placed,
        out_specs=placed,
        check_vma=False,
    )
```

```python
import functools
import math

import jax
import jax.numpy as jnp
from jax import lax
from jax.experimental import pallas as pl
from jax.experimental.pallas import tpu as pltpu
from jax.sharding import PartitionSpec as P

D = 2048
NS_ITERS = 4
CHUNKS = (2, 2, 2)
VMEM_LIMIT = 24 * 1024 * 1024

beta_one = 0.9
beta_two = 0.999
bias_one = 1.0 - 0.9**10
bias_two = 1.0 - 0.999**10
eps_adam = 1e-08
galore_gain = 4.0
width_root = math.sqrt(D)

F32 = jnp.float32
BF16 = jnp.bfloat16


def dot_tn(a, b):
    return lax.dot_general(a, b, (((0,), (0,)), ((), ())), preferred_element_type=F32)


def dot_nn(a, b):
    return lax.dot_general(a, b, (((1,), (0,)), ((), ())), preferred_element_type=F32)


def dot_nt(a, b):
    return lax.dot_general(a, b, (((1,), (1,)), ((), ())), preferred_element_type=F32)


def split(a):
    high = a.astype(BF16)
    return high, (a - high.astype(F32)).astype(BF16)


def fine(dot, a, b):
    (ah, al), (bh, bl) = a, b
    return dot(ah, bh) + (dot(ah, bl) + dot(al, bh))


def call(body, grid, prefetch, ins, outs, scratch, aliases=None, vmem=VMEM_LIMIT):
    return pl.pallas_call(
        body,
        grid_spec=pltpu.PrefetchScalarGridSpec(
            num_scalar_prefetch=1,
            grid=grid,
            in_specs=[
                pl.BlockSpec(memory_space=pl.ANY) if b is None else pl.BlockSpec(b, m)
                for _, b, m in ins
            ],
            out_specs=[pl.BlockSpec(b, m) for _, _, b, m in outs],
            scratch_shapes=scratch,
        ),
        out_shape=[jax.ShapeDtypeStruct(s, d) for s, d, _, _ in outs],
        input_output_aliases=aliases or {},
        compiler_params=pltpu.CompilerParams(vmem_limit_bytes=vmem),
        cost_estimate=pl.CostEstimate(flops=1, bytes_accessed=1, transcendentals=0),
    )(prefetch, *[a for a, _, _ in ins])


def outgoing(place, gradient, k0, kc, tensors):
    rows, columns = gradient.shape[1:]
    width = columns // tensors
    n = tensors - 1

    def body(place_ref, *refs):
        for m in range(n):
            refs[n + m][...] = refs[m][...]

    return call(
        body,
        (kc,),
        place,
        [
            (gradient, (1, rows, width), lambda i, p, m=m: (k0 + i, 0, jnp.bitwise_xor(p[0], m)))
            for m in range(1, tensors)
        ],
        [((kc, rows, width), BF16, (1, rows, width), lambda i, p: (i, 0, 0))] * n,
        [],
    )


def gradient_ins(gradient, got, k0, pick=lambda i, p: i):
    kc, rows, width = got[0].shape
    return [(gradient, (1, rows, width), lambda i, p: (k0 + pick(i, p), 0, p[0]))] + [
        (g, (1, rows, width), lambda i, p: (pick(i, p), 0, 0)) for g in got
    ]


def basis_ins(bases, k0):
    return [
        (a, (1,) + a.shape[1:], lambda i, p, n=a.shape[0]: (lax.rem(k0 + i, n), 0, 0))
        for group in bases
        for a in group
    ]


def basis_blocks(refs, bases, k0, core):
    refs = list(refs)
    blocks = []
    for group in bases:
        mine = refs.pop(0)[0]
        if len(group) == 2:
            owner = (k0 + pl.program_id(0)) // group[0].shape[0]
            mine = jnp.where(owner == core, mine, refs.pop(0)[0])
        blocks.append(mine)
    return blocks


def low_partial(place, gradient, bases, got, k0, sections):
    kc, rows, width = got[0].shape
    rank = bases[0][0].shape[2]
    part = width // sections
    n = len(bases)
    chosen = blocks_sent(sections)

    def body(place_ref, *refs):
        out, total = refs[-1 - len(chosen) : -1], refs[-1]
        blocks = basis_blocks(refs[n:], bases, k0, place_ref[2])
        acc = dot_tn(refs[0][0], blocks[0])
        for m in range(1, n):
            acc += dot_tn(refs[m][0], blocks[m])
        total[...] = acc
        z = place_ref[1]
        for j, block in enumerate(chosen):
            at = pl.multiple_of(block(z) * part, part)
            out[j][0] = total[pl.ds(at, part), :].astype(out[j].dtype)

    return call(
        body,
        (kc,),
        place,
        gradient_ins(gradient, got, k0) + basis_ins(bases, k0),
        [
            ((kc, part, rank), BF16 if j else F32, (1, part, rank), lambda i, p: (i, 0, 0))
            for j in range(len(chosen))
        ],
        [pltpu.VMEM((width, rank), F32)],
    )


def blocks_sent(sections):
    return [lambda z, m=m: jnp.bitwise_xor(z, m) for m in range(sections)]


def gather_into(whole, refs, gathered, z):
    refs = list(refs)
    part = refs[0].shape[-2]
    for j, group in enumerate(gathered):
        block = refs.pop(0)[0, 0]
        for _ in group[1:]:
            block = block + refs.pop(0)[0, 0]
        at = pl.multiple_of(jnp.bitwise_xor(z, j) * part, part)
        whole[pl.ds(at, part), :] = block


def update(place, terms, moment_m, moment_v, before, k0, joined):
    kc, part, rank = terms[0].shape
    n = len(terms)

    def body(place_ref, *refs):
        m_ref, v_ref = refs[n], refs[n + 1]
        *low_out, m_out, v_out = refs[-4 + joined :]
        total = refs[0][0]
        for j in range(1, n):
            total += refs[j][0].astype(F32)
        low_rank = total / width_root
        m_new = beta_one * m_ref[0] + (1.0 - beta_one) * low_rank
        v_new = beta_two * v_ref[0] + (1.0 - beta_two) * low_rank * low_rank
        step = m_new / bias_one / (jnp.sqrt(v_new / bias_two) + eps_adam)
        low_out[0][0, 0] = low_rank.astype(BF16)
        low_out[-1][int(joined), 0] = step.astype(BF16)
        m_out[0] = m_new
        v_out[0] = v_new

    here = lambda i, p: (k0 + i, 0, 0)
    block = (1, part, rank)
    ins = [(a, block, lambda i, p: (i, 0, 0)) for a in terms]
    ins += [(moment_m, block, here), (moment_v, block, here)]
    aliases = {}
    if before is not None:
        ins += [(b, None, None) for b in before]
        aliases = {n + 3: 2 - joined, n + 4: 3 - joined}
    return call(
        body,
        (kc,),
        place,
        ins,
        [
            (
                (1 + joined, kc, part, rank),
                BF16,
                (1 + joined, 1, part, rank),
                lambda i, p: (0, i, 0, 0),
            )
        ]
        * (2 - joined)
        + [
            (moment_m.shape, F32, block, here),
            (moment_v.shape, F32, block, here),
        ],
        [],
        aliases,
    )


def subspace_partial(place, gradient, got, gathered, k0, split_cores):
    kc, rows, width = got[0].shape
    flat = [r for group in gathered for r in group]
    part, rank = flat[0].shape[2:]
    n, s = len(got) + 1, len(flat)
    half = kc // 2

    def pick(i, p):
        if not split_cores:
            return i
        return jnp.where(i < half, 2 * i + p[2], 2 * (i - half) + 1 - p[2])

    def body(place_ref, *refs):
        out, whole = refs[-2:]
        gather_into(whole, refs[n : n + s], gathered, place_ref[1])
        for m in range(n):
            out[0, m] = dot_nn(refs[m][0], whole[...])

    return call(
        body,
        (kc,),
        place,
        gradient_ins(gradient, got, k0, pick)
        + [(r, (1, 1, part, rank), lambda i, p: (0, pick(i, p), 0, 0)) for r in flat],
        [((kc, n, rows, rank), F32, (1, n, rows, rank), lambda i, p: (i, 0, 0, 0))],
        [pltpu.VMEM((width, rank), BF16)],
    )[0]


def delta_parts(place, bases, gathered, k0):
    flat = [r for group in gathered for r in group]
    kc, part, rank = flat[0].shape[1:]
    rows = bases[0][0].shape[1]
    n, s = len(bases), len(flat)
    width = part * len(gathered)

    def body(place_ref, *refs):
        out, whole = refs[-1 - n : -1], refs[-1]
        gather_into(whole, refs[:s], gathered, place_ref[1])
        blocks = basis_blocks(refs[s:], bases, k0, place_ref[2])
        for m in range(n):
            out[m][0] = (-galore_gain / width_root * dot_nt(blocks[m], whole[...])).astype(BF16)

    return call(
        body,
        (kc,),
        place,
        [(r, (1, 1, part, rank), lambda i, p: (0, i, 0, 0)) for r in flat]
        + basis_ins(bases, k0),
        [((kc, rows, width), BF16, (1, rows, width), lambda i, p: (i, 0, 0))] * n,
        [pltpu.VMEM((width, rank), BF16)],
    )


def place_delta(place, parts, before, k0, matrices):
    kc, rows, width = parts[0].shape
    n = len(parts)

    def body(place_ref, *refs):
        out = refs[-1]
        for m in range(n):
            at = pl.multiple_of(jnp.bitwise_xor(place_ref[0], m) * width, width)
            out[0, :, pl.ds(at, width)] = refs[m][0]

    ins = [(p, (1, rows, width), lambda i, p: (i, 0, 0)) for p in parts]
    aliases = {}
    if before is not None:
        ins.append((before, None, None))
        aliases = {n + 1: 0}
    shape = (matrices, rows, n * width)
    return call(
        body,
        (kc,),
        place,
        ins,
        [(shape, BF16, (1, rows, n * width), lambda i, p: (k0 + i, 0, 0))],
        [],
        aliases,
    )[0]


def gram_parts(place, groups):
    n = len(groups[0])
    rows, rank = groups[0][0].shape[1:]
    counts = [g[0].shape[0] for g in groups]
    total = sum(counts)
    part = rank // n
    flat = [p for g in groups for p in g]

    def body(place_ref, *refs):
        pieces, sub, out, whole = refs[: len(flat)], refs[len(flat)], refs[len(flat) + 1 : -1], refs[-1]
        at = 0
        for j, count in enumerate(counts):
            for i in range(count):
                acc = pieces[j * n][i]
                for m in range(1, n):
                    acc += pieces[j * n + m][i]
                sub[at] = acc
                high = split(acc)
                whole[at] = fine(dot_tn, high, high)
                at += 1
        for m in range(n):
            start = pl.multiple_of(jnp.bitwise_xor(place_ref[0], m) * part, part)
            for i in range(total):
                out[m][i] = whole[i, pl.ds(start, part), :]

    zero3 = lambda i, p: (0, 0, 0)
    res = call(
        body,
        (1,),
        place,
        [(p, p.shape, zero3) for p in flat],
        [((total, rows, rank), F32, (total, rows, rank), zero3)]
        + [((total, part, rank), F32, (total, part, rank), zero3)] * n,
        [pltpu.VMEM((total, rank, rank), F32)],
    )
    return res[0], res[1:]


def newton_schulz(place, pieces, sub):
    n = len(pieces)
    total, rows, rank = sub.shape
    part = rank // n

    def body(place_ref, *refs):
        p, s, out, whole = refs[:n], refs[n], refs[n + 1], refs[-1]
        for m in range(n):
            start = pl.multiple_of(jnp.bitwise_xor(place_ref[0], m) * part, part)
            for i in range(total):
                whole[i, pl.ds(start, part), :] = p[m][i]
        row = lax.broadcasted_iota(jnp.int32, (rank, rank), 0)
        col = lax.broadcasted_iota(jnp.int32, (rank, rank), 1)
        eye = jnp.where(row == col, 1.0, 0.0).astype(F32)
        iters, grams, prods = [], [], []
        for i in range(total):
            gram = whole[i]
            bound = jnp.max(jnp.sum(jnp.abs(gram), axis=1, keepdims=True), axis=0, keepdims=True) + 1e-06
            iters.append(s[i] / jnp.sqrt(bound))
            grams.append(gram / bound)
            prods.append(None)
        for turn in range(NS_ITERS):
            for i in range(total):
                factor = 1.5 * eye - 0.5 * grams[i]
                f = split(factor)
                prods[i] = factor if turn == 0 else fine(dot_nn, split(prods[i]), f)
                if turn + 1 < NS_ITERS:
                    half = fine(dot_nn, split(grams[i]), f)
                    grams[i] = fine(dot_nn, split(half), f)
        for i in range(total):
            res = fine(dot_nn, split(iters[i]), split(prods[i]))
            out[i] = (width_root * res).astype(BF16)

    zero3 = lambda i, p: (0, 0, 0)
    return call(
        body,
        (1,),
        place,
        [(p, p.shape, zero3) for p in pieces] + [(sub, sub.shape, zero3)],
        [((total, rows, rank), BF16, (total, rows, rank), zero3)],
        [pltpu.VMEM((total, rank, rank), F32)],
    )[0]


def after(x, *others):
    return lax.optimization_barrier((x, others))[0]


def per_device(shape, gradient, basis, moment_m, moment_v):
    tensors, sections, cores = shape["tensor"], shape["section"], shape["shard"]
    t, z, c = (lax.axis_index(a) for a in ("tensor", "section", "shard"))
    place = jnp.stack([t, z, c]).astype(jnp.int32)
    matrices = gradient.shape[0]
    split_cores = cores == 2
    n = len(CHUNKS)
    starts = [sum(CHUNKS[:j]) for j in range(n)]

    def swap(x, axis, m):
        return lax.ppermute(x, axis, [(i, i ^ m) for i in range(shape[axis])])

    token = ()

    def event(*values):
        nonlocal token, place
        token = values
        place = after(place, *values)

    def send(x, axis, m):
        return swap(after(x, *token), axis, m)

    def other_core(x):
        return lax.ppermute(after(x, *token), "shard", [(0, 1), (1, 0)])

    def send_all(cut):
        return [send(cut[m - 1], "tensor", m) for m in range(1, tensors)]

    grads, parts, sums, roughs, steps, cuts, subs, groups = ({} for _ in range(8))
    state = {"news": None, "delta": None}
    wide = sections != 4

    def cut(j):
        cuts[j] = outgoing(place, gradient, starts[j], CHUNKS[j], tensors)
        event(*cuts[j])

    def send_grads(j):
        grads[j] = send_all(cuts[j])

    def wait_grads(j):
        event(*grads[j])

    def low(j):
        parts[j] = low_partial(place, gradient, bases, grads[j], starts[j], sections)
        event(*parts[j])

    def sum_far(j):
        sums[j] = [parts[j][0]] + [None] * (sections - 1)
        if wide:
            sums[j][1:] = [send(x, "section", m + 1) for m, x in enumerate(parts[j][1:])]
        else:
            sums[j][2] = send(parts[j][3], "section", 1)
            sums[j].pop()

    def sum_near(j):
        if not wide:
            sums[j][1] = send(parts[j][1], "section", 1)

    def sum_two(j):
        if not wide:
            event(sums[j][2])
            both = parts[j][2].astype(F32) + sums[j][2].astype(F32)
            sums[j][2] = send(both.astype(BF16), "section", 2)

    def step(j):
        event(*sums[j])
        *low_out, m_new, v_new = update(
            place, sums[j], moment_m, moment_v, state["news"], starts[j], False
        )
        state["news"] = [m_new, v_new]
        roughs[j], steps[j] = [[[x]] + [None] * (sections - 1) for x in low_out]
        event(*low_out)

    def gather_two(held):
        if wide:
            held[1:] = [[send(held[0][0], "section", m)] for m in range(1, sections)]
        else:
            held[2] = [send(held[0][0], "section", 2)]

    def gather_near(held):
        if not wide:
            held[1] = [send(held[0][0], "section", 1)]

    def gather_far(held):
        if not wide:
            event(held[2][0])
            held[3] = [send(held[2][0], "section", 1)]

    def hop(x, pairs):
        return lax.ppermute(after(x, *token), "section", pairs)

    inwards, across, outwards = ((0, 1), (3, 2)), ((1, 2), (2, 1)), ((1, 0), (2, 3))

    def sum_in(j):
        sums[j] = {"own": parts[j][0]}
        if wide:
            sums[j]["all"] = [send(x, "section", m + 1) for m, x in enumerate(parts[j][1:])]
        else:
            sums[j]["end"] = hop(parts[j][3], inwards)

    def sum_in_two(j):
        if not wide:
            sums[j]["inner"] = hop(parts[j][2], inwards)

    def merged(x, y):
        return (x.astype(F32) + y.astype(F32)).astype(BF16)

    def sum_across(j):
        if not wide:
            event(sums[j]["end"])
            sums[j]["end"] = hop(merged(parts[j][2], sums[j]["end"]), across)

    def sum_across_two(j):
        if not wide:
            event(sums[j]["inner"])
            sums[j]["inner"] = hop(merged(parts[j][3], sums[j]["inner"]), across)

    def sum_out(j):
        if wide:
            sums[j] = [sums[j]["own"]] + sums[j]["all"]
        else:
            event(sums[j]["end"])
            last = send(merged(parts[j][1], sums[j]["end"]), "section", 1)
            sums[j] = [sums[j]["own"], sums[j]["inner"], last]

    def spread_across(held):
        if not wide:
            held[3] = [hop(held[0][0], across)]

    def spread_across_two(held):
        if not wide:
            event(held[1][0])
            held[2] = [hop(held[1][0], across)]

    def spread_out(held):
        if not wide:
            event(held[3][0])
            held[2].append(hop(held[3][0], outwards))

    def spread_out_two(held):
        if wide:
            gather_two(held)
        else:
            event(held[2][0])
            held[3].append(hop(held[2][0], outwards))

    def rough_across(j):
        spread_across(roughs[j])

    def rough_across_two(j):
        spread_across_two(roughs[j])

    def rough_out(j):
        spread_out(roughs[j])

    def rough_out_two(j):
        spread_out_two(roughs[j])

    def step_across(j):
        spread_across(steps[j])

    def step_across_two(j):
        spread_across_two(steps[j])

    def step_out(j):
        spread_out(steps[j])

    def step_out_two(j):
        spread_out_two(steps[j])

    def rough_two(j):
        gather_two(roughs[j])

    def rough_near(j):
        gather_near(roughs[j])

    def rough_far(j):
        gather_far(roughs[j])

    def step_two(j):
        gather_two(steps[j])

    def step_near(j):
        gather_near(steps[j])

    def step_far(j):
        gather_far(steps[j])

    def subspace(j):
        event(roughs[j])
        subs[j] = subspace_partial(place, gradient, grads[j], roughs[j], starts[j], split_cores)
        event(subs[j])

    def share(j):
        if split_cores:
            groups[j] = other_core(subs[j][CHUNKS[j] // 2 :])
        else:
            groups[j] = lax.psum(subs[j], "shard")

    def spread(j):
        event(groups[j])
        total = groups[j]
        if split_cores:
            total = total + subs[j][: CHUNKS[j] // 2]
        groups[j] = [total[:, 0]] + [send(total[:, m], "tensor", m) for m in range(1, tensors)]

    def wait_spread(j):
        event(*groups[j])

    def delta(j):
        event(steps[j])
        cuts[j] = delta_parts(place, bases, steps[j], starts[j])
        event(*cuts[j])

    def send_delta(j):
        cuts[j] = [cuts[j][0]] + send_all(cuts[j][1:])

    def put(j):
        event(*cuts[j])
        state["delta"] = place_delta(place, cuts[j], state["delta"], starts[j], matrices)
        event(state["delta"])

    def fetch():
        mine = basis
        if split_cores:
            mine = lax.dynamic_slice_in_dim(basis, c * (matrices // 2), matrices // 2, 0)
            event(mine)
        bases.extend([send(mine, "tensor", m)] for m in range(1, tensors))

    def hand_over():
        if split_cores:
            event(*[group[0] for group in bases[1:]])
            for group in bases[1:]:
                group.append(other_core(group[0]))

    def gram_kernel():
        state["sub"], state["gram"] = gram_parts(place, [groups[j] for j in range(n)])
        event(*state["gram"])

    def gram_send():
        cut = state["gram"]
        state["gram"] = [cut[0]] + send_all(cut[1:])

    def gram_sum():
        event(*state["gram"])
        state["gram"] = functools.reduce(jnp.add, state["gram"])
        state["reach"] = 1

    def gram_hop():
        state["hop"] = send(state["gram"], "section", state["reach"])
        state["reach"] *= 2

    def gram_add():
        event(state["hop"])
        state["gram"] = state["gram"] + state["hop"]

    def gram_gather():
        gram = state["gram"]
        state["gram"] = [gram] + [send(gram, "tensor", m) for m in range(1, tensors)]

    def newton():
        event(*state["gram"])
        state["done"] = newton_schulz(place, state["gram"], state["sub"])
        event(state["done"])

    def finish():
        done = state["done"]
        if split_cores:
            theirs = other_core(done)
            even = jnp.where(c == 0, done, theirs)
            odd = jnp.where(c == 0, theirs, done)
            done = jnp.stack([even, odd], 1).reshape(basis.shape)
        state["done"] = done

    bases = [[basis]]
    fetch()
    cut(0)
    hand_over()
    send_grads(0)
    cut(1)
    wait_grads(0)
    send_grads(1)
    low(0)
    sum_far(0)
    sum_near(0)
    sum_two(0)
    cut(2)
    step(0)
    rough_two(0)
    send_grads(2)
    wait_grads(1)
    rough_near(0)
    low(1)
    step_two(0)
    sum_far(1)
    rough_far(0)
    sum_near(1)
    sum_two(1)
    subspace(0)
    share(0)
    step_near(0)
    step(1)
    wait_grads(2)
    step_far(0)
    rough_across(1)
    rough_near(1)
    low(2)
    sum_far(2)
    sum_near(2)
    rough_across_two(1)
    sum_two(2)
    delta(0)
    send_delta(0)
    rough_out(1)
    step(2)
    step_near(1)
    rough_out_two(1)
    rough_two(2)
    step_two(1)
    rough_far(2)
    spread(0)
    rough_near(2)
    subspace(1)
    share(1)
    subspace(2)
    put(0)
    share(2)
    step_far(1)
    spread(1)
    step_two(2)
    step_near(2)
    spread(2)
    wait_spread(1)
    delta(1)
    wait_spread(0)
    send_delta(1)
    wait_spread(2)
    gram_kernel()
    gram_send()
    step_far(2)
    gram_sum()
    gram_hop()
    put(1)
    gram_add()
    gram_hop()
    gram_add()
    gram_gather()
    delta(2)
    newton()
    send_delta(2)
    finish()
    put(2)
    return (state["delta"], state["done"], *state["news"])


def solution(mesh):
    placed = (
        P(None, ("tensor", "section"), "shard"),
        P(None, ("tensor", "section"), None),
        P(None, ("shard", "tensor", "section"), None),
        P(None, ("shard", "tensor", "section"), None),
    )
    return jax.shard_map(
        functools.partial(per_device, dict(mesh.shape)),
        mesh=mesh,
        in_specs=placed,
        out_specs=placed,
        check_vma=False,
    )
```
